128 devices in a mesh: dp: 16 (over x, z), tensor: 8 (over y, core).
Axes of the slice: x: 4, y: 4, z: 4, core: 2. Of those that a mesh axis runs over, the one named last changes fastest.
Arguments:
- tokens: bfloat16 [16384, 2560], P(('dp', 'tensor')), may hold values from -6 to 6
- out_grad: bfloat16 [16384, 2560], P(('dp', 'tensor')), may hold values from -0.75 to 0.75
- routing: int32 [16384, 1], P(('dp', 'tensor')), may hold values from 0 to 15; in each aligned block of 128 rows (0 to 127, 128 to 255, ...) at most 12 rows name the same one
- router_weight: bfloat16 [2560, 16], replicated, may hold values from -0.125 to 0.125
- gate_weight: bfloat16 [16, 2560, 4096], P('dp', None, 'tensor'), may hold values from -0.125 to 0.125
- up_weight: bfloat16 [16, 2560, 4096], P('dp', None, 'tensor'), may hold values from -0.125 to 0.125
- down_weight: bfloat16 [16, 4096, 2560], P('dp', 'tensor'), may hold values from -0.09375 to 0.09375
- saved_gate: bfloat16 [16, 1536, 4096], P('dp', None, 'tensor'), may hold values from -6 to 6
- saved_up: bfloat16 [16, 1536, 4096], P('dp', None, 'tensor'), may hold values from -6 to 6
Outputs:
- grad_tokens: bfloat16 [16384, 2560], P(('dp', 'tensor'))
- grad_gate: bfloat16 [16, 2560, 4096], P('dp', None, 'tensor')
- grad_up: bfloat16 [16, 2560, 4096], P('dp', None, 'tensor')
- grad_down: bfloat16 [16, 4096, 2560], P('dp', 'tensor')
- grad_router: float32 [2560, 16], replicated
The draws below stay inside these ranges and needn't reach their ends.
Inputs may be any that keep to these rules, and one draw needn't show every extreme that they name: `routing`: within the 128 rows of one device no expert is named by more than 12 rows; in every draw some device's rows name some expert exactly 12 times.
All inputs are finite; a program needn't handle non-finite values.
Results may differ from the reference program's by a relative error of at most 0.015.
Values may be sent and summed in bfloat16 or wider, within the bound.
A program may use at most 192 MiB of HBM per device.

```python
import math
import jax
import jax.numpy as jnp
import numpy as np
from jax import lax

D = 2560
FF = 4096
TOK_DEV = 128
EXPERTS = 16
CAP = 12
SLOTS = 1536
TOKENS = 16384
N_TENSOR = 8


def block_levels(own_key, dims, split, smallest, largest):
    factor_of = 1.0
    for axis_at, blocks in split:
        heights = jax.random.uniform(jax.random.fold_in(jax.random.fold_in(own_key, 6), axis_at), (blocks,), jnp.float32, smallest / len(split), largest / len(split))
        factor_of = factor_of * jnp.repeat(jnp.exp(heights), dims[axis_at] // blocks).reshape((-1,) + (1,) * (len(dims) - 1 - axis_at))
    return factor_of


def routed_block(own_key, own, number, rows, count, top, reach, slope):
    sequence = jax.random.permutation(own_key, count)
    crowded, common = load_shares(count, rows * top, reach, slope, True), load_shares(count, rows * top, reach, slope, False)
    places = jnp.arange(count)

    def named(sizes, rotation):
        used = int((sizes > 0).sum())
        fixed = max(1, used // 4)
        passed = fixed + (places - fixed + rotation * (used - fixed)) % max(1, count - fixed)
        return jnp.zeros((count,), jnp.int32).at[sequence[jnp.where(places < fixed, places, passed)]].set(jnp.asarray(sizes, jnp.int32))

    sizes = jnp.where(number % 4 == 0, named(crowded, number // 4), named(common, number - number // 4 - 1))
    mixed = jax.random.permutation(jax.random.fold_in(own, 3), count)
    donor, receiver = mixed[0:count // 2 * 2:2], mixed[1:count // 2 * 2:2]
    slack = jnp.minimum(sizes[donor] - 1, reach - sizes[receiver]) // 2
    slack = jnp.where((donor == sequence[0]) | (receiver == sequence[0]) | (sizes[receiver] == 0), 0, jnp.maximum(slack, 0))
    passed = jax.random.randint(jax.random.fold_in(own, 4), (count // 2,), 0, 1 << 20) % (slack + 1)
    sizes = sizes.at[donor].add(-passed).at[receiver].add(passed)
    labels = jnp.searchsorted(jnp.cumsum(sizes), jnp.arange(rows * top), side="right").astype(jnp.int32)
    grid = labels.reshape(top, rows).T
    grid = grid[jax.random.permutation(jax.random.fold_in(own, 1), rows)]
    rotation = jax.random.randint(jax.random.fold_in(own, 2), (rows, 1), 0, top)
    return jnp.take_along_axis(grid, (jnp.arange(top)[None, :] + rotation) % top, axis=1)


def load_shares(number_of, total, most, slope, full):
    portions = [(1 << 20) // math.isqrt(grade ** slope) + 1 for grade in range(1, number_of + 1)]
    largest = most if full else min(most, max(-(-total // number_of), total * portions[0] // sum(portions)))
    least = 1 if total - largest >= number_of - 1 else 0
    given, rest = [largest] + [least] * (number_of - 1), total - largest - least * (number_of - 1)
    while rest > 0:
        movable = [i for i in range(1, number_of) if given[i] < largest] or [i for i in range(1, number_of) if given[i] < most]
        pool, budget = sum([portions[i] for i in movable]), rest
        for i in movable:
            extra = min(most - given[i], max(1, budget * portions[i] // pool), rest)
            given[i] = given[i] + extra
            rest = rest - extra
    return np.array(given)


def normal_values(rng, extent, deviation, limit, shards=(), kind=jnp.bfloat16):
    entries = deviation * jax.random.normal(rng, extent, jnp.float32)
    if shards:
        entries = entries * block_levels(rng, extent, shards, -0.22, 0.18)
    return jnp.clip(entries, -limit, limit).astype(kind)


def setup_inputs(seed: int = 0) -> dict:
    key_list = jax.random.split(jax.random.key(seed), 10)
    tokens = normal_values(key_list[0], (TOKENS, D), 1.0, 6.0, ((0, 128),))
    out_grad = normal_values(key_list[1], (TOKENS, D), 0.125, 0.75, ((0, 128),))
    routing_keys = jax.random.split(jax.random.fold_in(key_list[2], 1), TOKENS // TOK_DEV)
    routing_turns = jax.random.permutation(jax.random.fold_in(key_list[2], 3), TOKENS // TOK_DEV)
    routing = jax.vmap(lambda own, number: routed_block(jax.random.fold_in(key_list[2], 2), own, number, TOK_DEV, EXPERTS, 1, CAP, 2))(routing_keys, routing_turns).reshape((TOKENS, 1))
    router_weight = normal_values(key_list[3], (D, EXPERTS), D ** -0.5, 0.125)
    gate_weight = normal_values(key_list[4], (EXPERTS, D, FF), D ** -0.5, 0.125, ((0, 16), (2, 8)))
    up_weight = normal_values(key_list[5], (EXPERTS, D, FF), D ** -0.5, 0.125, ((0, 16), (2, 8)))
    down_weight = normal_values(key_list[6], (EXPERTS, FF, D), FF ** -0.5, 0.09375, ((0, 16), (1, 8)))
    saved_gate = normal_values(key_list[7], (EXPERTS, SLOTS, FF), 1.0, 6.0, ((0, 16), (2, 8)))
    saved_up = normal_values(key_list[8], (EXPERTS, SLOTS, FF), 1.0, 6.0, ((0, 16), (2, 8)))
    return {"tokens": tokens, "out_grad": out_grad, "routing": routing, "router_weight": router_weight, "gate_weight": gate_weight, "up_weight": up_weight, "down_weight": down_weight, "saved_gate": saved_gate, "saved_up": saved_up}


def one_expert(items):
    routed_x, routed_g, gate_w, up_w, down_w, gate_pre, up_pre = items
    gate_f = gate_pre.astype(jnp.float32)
    up_f = up_pre.astype(jnp.float32)
    sigmoid_a = jax.nn.sigmoid(gate_f)
    silu_a = gate_f * sigmoid_a
    hidden = (silu_a * up_f).astype(jnp.bfloat16)
    grad_hidden = jnp.dot(routed_g, down_w.T, preferred_element_type=jnp.float32)
    grad_a = (grad_hidden * up_f * sigmoid_a * (1.0 + gate_f * (1.0 - sigmoid_a))).astype(jnp.bfloat16)
    grad_b = (grad_hidden * silu_a).astype(jnp.bfloat16)
    down_out = jnp.dot(hidden.T, routed_g, preferred_element_type=jnp.float32).astype(jnp.bfloat16)
    gate_out = jnp.dot(routed_x.T, grad_a, preferred_element_type=jnp.float32).astype(jnp.bfloat16)
    up_out = jnp.dot(routed_x.T, grad_b, preferred_element_type=jnp.float32).astype(jnp.bfloat16)
    group_width = FF // N_TENSOR

    def add_group(group, total):
        start = (group * group_width).astype(jnp.int32)
        term = jnp.dot(lax.dynamic_slice_in_dim(grad_a, start, group_width, 1),
                       lax.dynamic_slice_in_dim(gate_w, start, group_width, 1).T,
                       preferred_element_type=jnp.float32)
        term = term + jnp.dot(lax.dynamic_slice_in_dim(grad_b, start, group_width, 1),
                              lax.dynamic_slice_in_dim(up_w, start, group_width, 1).T,
                              preferred_element_type=jnp.float32)
        rounded = lax.optimization_barrier(term.astype(jnp.bfloat16))
        return total + rounded.astype(jnp.float32)

    summed = lax.fori_loop(0, N_TENSOR, add_group, jnp.zeros((SLOTS, D), jnp.float32))
    return summed.astype(jnp.bfloat16), gate_out, up_out, down_out


def reference(tokens, out_grad, routing, router_weight, gate_weight, up_weight, down_weight, saved_gate, saved_up):
    chosen = routing[:, 0]
    sources = TOKENS // TOK_DEV
    onehot = (chosen[:, None] == jnp.arange(EXPERTS, dtype=jnp.int32)[None, :]).astype(jnp.int32)
    blocks = onehot.reshape(sources, TOK_DEV, EXPERTS)
    earlier = jnp.cumsum(blocks, axis=1) - blocks
    slot_index = jnp.sum(earlier * blocks, axis=2).reshape(TOKENS)
    source = jnp.arange(TOKENS, dtype=jnp.int32) // TOK_DEV
    target_row = (source * CAP + slot_index).astype(jnp.int32)
    onehot_float = onehot.astype(jnp.float32)
    logits = jnp.dot(tokens, router_weight, preferred_element_type=jnp.float32)
    gate_score = jax.nn.sigmoid(jnp.sum(logits * onehot_float, axis=1))
    scaled = (gate_score[:, None] * tokens.astype(jnp.float32)).astype(jnp.bfloat16)
    routed_in = jnp.zeros((EXPERTS, SLOTS, D), jnp.bfloat16).at[chosen, target_row].set(scaled)
    routed_grad = jnp.zeros((EXPERTS, SLOTS, D), jnp.bfloat16).at[chosen, target_row].set(out_grad)
    grad_in, grad_gate, grad_up, grad_down = lax.map(
        one_expert, (routed_in, routed_grad, gate_weight, up_weight, down_weight, saved_gate, saved_up))
    grad_scaled = grad_in[chosen, target_row].astype(jnp.float32)
    grad_score = jnp.sum(tokens.astype(jnp.float32) * grad_scaled, axis=1)
    grad_logit = grad_score * gate_score * (1.0 - gate_score)
    picked = router_weight.T[chosen].astype(jnp.float32)
    grad_tokens = (gate_score[:, None] * grad_scaled + grad_logit[:, None] * picked).astype(jnp.bfloat16)
    grad_router = jnp.dot(tokens.astype(jnp.float32).T, grad_logit[:, None] * onehot_float,
                          precision=lax.Precision.HIGHEST)
    return grad_tokens, grad_gate, grad_up, grad_down, grad_router
```

```python
import jax
import jax.numpy as jnp
from jax import lax
from jax.experimental import pallas as pl
from jax.experimental.pallas import tpu as pltpu
from jax.sharding import PartitionSpec as P

MESH = pl.DeviceIdType.MESH
NN = (((1,), (0,)), ((), ()))
NT = (((1,), (1,)), ((), ()))
F32 = jnp.float32
BF16 = jnp.bfloat16

CHUNKS = 3
GROUPS = 4


def mm(a, b, dims=NN):
    return lax.dot_general(a, b, dims, preferred_element_type=F32)


def iota(shape, dim):
    return lax.broadcasted_iota(jnp.int32, shape, dim)


def eye_mask(n):
    return iota((n, n), 0) == iota((n, n), 1)


def kernel(
    routing_ref,
    tokens_hbm,
    out_grad_hbm,
    router_hbm,
    gate_hbm,
    up_hbm,
    down_hbm,
    saved_gate_hbm,
    saved_up_hbm,
    grad_tokens_hbm,
    grad_gate_hbm,
    grad_up_hbm,
    grad_down_hbm,
    grad_router_ref,
    tok,
    ogr,
    scaled,
    rw,
    gate,
    up,
    down,
    a_perm,
    b_perm,
    hid_t,
    ga,
    gb,
    send_g,
    send_i,
    recv_g,
    recv_i,
    recv_r,
    full_g,
    full_i,
    send_c,
    own_p,
    recv_c,
    st1_s,
    st1_r,
    st2_s,
    st2_r,
    unfold_m,
    fold_m,
    save_m,
    eye_m,
    gs,
    tgt_row,
    cols,
    rp_s,
    rp_r,
    rd_s,
    rd_r,
    ro_s,
    ro_r,
    load_sem,
    a2a_s,
    a2a_r,
    ag_s,
    ag_r,
    pc_s,
    pc_r,
    rs_s,
    rs_r,
    rt_s,
    rt_r,
    out_sem,
):
    d = lax.axis_index("dp")
    t = lax.axis_index("tensor")
    y = t // 2
    c = lax.rem(t, 2)
    right = (d, lax.rem(y + 1, 4) * 2 + c)
    left = (d, lax.rem(y + 3, 4) * 2 + c)
    partner = (d, y * 2 + 1 - c)
    mine = c * 4 + y
    from_left = c * 4 + lax.rem(y + 3, 4)
    from_right = c * 4 + lax.rem(y + 1, 4)
    far = c * 4 + lax.rem(y + 2, 4)
    dgw = tok.shape[1] // GROUPS
    rows = full_g.shape[1] * full_g.shape[2]
    width = tok.shape[1]

    loads = [
        pltpu.make_async_copy(src, dst, load_sem.at[n])
        for n, (src, dst) in enumerate(
            (
                (out_grad_hbm, ogr),
                (tokens_hbm, tok),
                (router_hbm, rw),
                (saved_gate_hbm, ga),
                (saved_up_hbm, gb),
                (down_hbm, down),
                (gate_hbm, gate),
                (up_hbm, up),
            )
        )
    ]
    for load in loads:
        load.start()

    barrier = pltpu.get_barrier_semaphore()

    @pl.loop(1, 16)
    def _(k):
        pl.semaphore_signal(
            barrier, inc=1, device_id=(lax.rem(d + k, 16), t), device_id_type=MESH
        )

    @pl.loop(1, 8)
    def _(k):
        pl.semaphore_signal(
            barrier, inc=1, device_id=(d, lax.rem(t + k, 8)), device_id_type=MESH
        )

    def remote(src, dst, send_sem, recv_sem, to):
        return pltpu.make_async_remote_copy(
            src_ref=src,
            dst_ref=dst,
            send_sem=send_sem,
            recv_sem=recv_sem,
            device_id=to,
            device_id_type=MESH,
        )

    def a2a_start(src, dst, kind, j):
        @pl.loop(1, 16)
        def _(k):
            to = lax.rem(d + k, 16)
            remote(
                src.at[j, to], dst.at[j, d], a2a_s.at[kind, j], a2a_r.at[kind, j], (to, t)
            ).start()

        dst[j, d] = src[j, d]

    def a2a_wait(dst, kind, j):
        part = dst.at[j, pl.ds(0, 15)]
        pltpu.make_async_copy(part, part, a2a_r.at[kind, j]).wait()

    def a2a_drain(src, kind, j):
        part = src.at[j, pl.ds(0, 15)]
        pltpu.make_async_copy(part, part, a2a_s.at[kind, j]).wait()

    def gather_copy(buf, kind, j, n):
        block, to = (
            (buf.at[j, mine], right),
            (buf.at[j, mine], left),
            (buf.at[j, from_left, pl.ds(0, 32)], right),
            (buf.at[j, from_right, pl.ds(32, 32)], left),
            (buf.at[j, mine], partner),
            (buf.at[j, from_left], partner),
            (buf.at[j, from_right], partner),
            (buf.at[j, far], partner),
        )[n]
        return remote(block, block, ag_s.at[kind, j, n], ag_r.at[kind, j, n], to)

    def gather_own(buf, kind, j):
        for n in (0, 1, 4):
            gather_copy(buf, kind, j, n).start()

    def landed(buf, kind, j, n):
        other = (1 - c) * 4
        block = (
            lambda: buf.at[j, from_left],
            lambda: buf.at[j, from_right],
            lambda: buf.at[j, far, pl.ds(0, 32)],
            lambda: buf.at[j, far, pl.ds(32, 32)],
            lambda: buf.at[j, other + y],
            lambda: buf.at[j, other + lax.rem(y + 3, 4)],
            lambda: buf.at[j, other + lax.rem(y + 1, 4)],
            lambda: buf.at[j, other + lax.rem(y + 2, 4)],
        )[n]()
        remote(block, block, ag_s.at[kind, j, n], ag_r.at[kind, j, n], partner).wait_recv()

    def gather_near(buf, kind, j):
        landed(buf, kind, j, 0)
        gather_copy(buf, kind, j, 2).start()
        gather_copy(buf, kind, j, 5).start()
        landed(buf, kind, j, 1)
        gather_copy(buf, kind, j, 3).start()
        gather_copy(buf, kind, j, 6).start()

    def gather_far(buf, kind, j):
        landed(buf, kind, j, 2)
        landed(buf, kind, j, 3)
        gather_copy(buf, kind, j, 7).start()

    def gather_rest(buf, kind, j):
        for n in (4, 5, 6, 7):
            landed(buf, kind, j, n)

    e_row = routing_ref[...]
    expert_t = iota((16, 128), 0) == e_row
    onehot_t = expert_t.astype(F32)
    before = (iota((128, 128), 0) < iota((128, 128), 1)).astype(BF16)
    earlier = mm(onehot_t.astype(BF16), before)
    slot = jnp.sum(earlier * onehot_t, axis=0, keepdims=True)
    high = (slot >= 4.0).astype(F32) + (slot >= 8.0).astype(F32)
    e_float = e_row.astype(F32)
    target = high * 252.0 + e_float * 16.0 + slot
    tgt_row[...] = target.astype(jnp.int32)
    eye128 = eye_mask(128)

    def to_column(row):
        return jnp.sum(jnp.where(eye128, row, 0.0), axis=1, keepdims=True)

    def to_row(column):
        return jnp.sum(jnp.where(eye128, column, 0.0), axis=0, keepdims=True)

    cols[0] = jnp.broadcast_to(to_column(target), (128, 128))
    cols[1] = jnp.broadcast_to(to_column(e_float), (128, 128))

    def fold_tokens(src, dst, j):
        total = None
        for g in range(GROUPS):
            place = (iota((256, 128), 0) == tgt_row[...] + (4 * g - 256 * j)).astype(BF16)
            term = mm(place, src[:, g * dgw : (g + 1) * dgw])
            total = term if total is None else total + term
        dst[j] = total.astype(BF16).reshape(16, 16, dgw)

    out_at = iota((256, 256), 0)
    in_at = iota((256, 256), 1)
    unfold_m[...] = (
        in_at == ((out_at >> 2) & 15) * 16 + (out_at >> 6) * 4 + (out_at & 3)
    ).astype(BF16)
    fold_m[...] = (
        in_at == ((out_at >> 2) & 3) * 64 + (out_at >> 4) * 4 + (out_at & 3)
    ).astype(BF16)

    loads[0].wait()
    for j in range(CHUNKS):
        fold_tokens(ogr, send_g, j)
        if j == 0:
            pl.semaphore_wait(barrier, 22)
        a2a_start(send_g, recv_g, 0, j)

    loads[1].wait()
    loads[2].wait()
    logits = mm(tok[...], rw[...])
    lane_e = iota((128, 16), 1).astype(F32)
    onehot = (lane_e == cols[1][:, :16]).astype(F32)
    score = jax.nn.sigmoid(jnp.sum(logits * onehot, axis=1, keepdims=True))
    cols[2] = jnp.broadcast_to(score, (128, 128))
    for g in range(GROUPS):
        part = slice(g * dgw, (g + 1) * dgw)
        scaled[:, part] = (score * tok[:, part].astype(F32)).astype(BF16)
    for j in range(CHUNKS):
        fold_tokens(scaled, send_i, j)
        a2a_start(send_i, recv_i, 1, j)

    save_out = iota((384, 384), 0)
    save_m[...] = (
        iota((384, 384), 1)
        == ((save_out >> 2) & 3) * 96
        + (((save_out >> 4) & 3) * 2 + ((save_out >> 6) & 1)) * 12
        + (save_out >> 7) * 4
        + (save_out & 3)
    ).astype(BF16)
    eye_m[...] = eye_mask(256).astype(BF16)
    loads[3].wait()
    loads[4].wait()

    def permute_saved(src, dst):
        @pl.loop(0, 4)
        def _(q):
            block = src[pl.ds(pl.multiple_of(q * 384, 384), 384), :]
            moved = mm(save_m[...], block).astype(BF16)
            for j in range(CHUNKS):
                for p in range(8):
                    start = (j * 8 + p) * 16
                    dst[j, pl.ds(pl.multiple_of(p * 64 + q * 16, 16), 16), :] = moved[
                        start : start + 16, :
                    ]

    permute_saved(ga, a_perm)
    permute_saved(gb, b_perm)

    def unfold(src, buf, j):
        moved = mm(unfold_m[...], src[j].reshape(256, dgw)).astype(BF16)
        for g in range(GROUPS):
            buf[j, mine, :, g * dgw : (g + 1) * dgw] = moved[g * 64 : (g + 1) * 64, :]

    def transposed(src_rows):
        return mm(eye_m[...], src_rows, NT).astype(BF16)

    def make_hidden(j):
        @pl.loop(0, 2)
        def _(n):
            at = pl.ds(pl.multiple_of(n * 256, 256), 256)
            a = a_perm[j, :, at].astype(F32)
            b = b_perm[j, :, at].astype(F32)
            hidden = (a * jax.nn.sigmoid(a) * b).astype(BF16)
            hid_t[j, at, :] = transposed(hidden)

    def compute(j):
        @pl.loop(0, 2)
        def _(n):
            at = pl.ds(pl.multiple_of(n * 256, 256), 256)
            gh = mm(full_g[j].reshape(rows, width), down[at, :], NT)
            a = a_perm[j, :, at].astype(F32)
            b = b_perm[j, :, at].astype(F32)
            sg = jax.nn.sigmoid(a)
            silu = a * sg
            here = pl.ds(j * 512, 512)
            ga[here, at] = (gh * b * sg * (1.0 + a * (1.0 - sg))).astype(BF16)
            gb[here, at] = (gh * silu).astype(BF16)

    def partial(j, parity, n):
        at = pl.ds(pl.multiple_of(j * 512 + parity * 256, 256), 256)
        hold = pl.ds(pl.multiple_of(n * dgw, 128), dgw)
        value = mm(ga[at, :], gate[hold, :], NT) + mm(gb[at, :], up[hold, :], NT)
        return value.astype(BF16).reshape(4, 64, dgw)

    def pair_copy(j):
        return remote(send_c, recv_c.at[j], pc_s.at[j], pc_r.at[j], partner)

    def partials(j):
        if j > 0:
            pair_copy(j - 1).wait_send()

        @pl.loop(0, GROUPS)
        def _(n):
            send_c[:, :, pl.ds(pl.multiple_of(n * dgw, 128), dgw)] = partial(j, 1 - c, n)

        pair_copy(j).start()

        @pl.loop(0, GROUPS)
        def _(n):
            own_p[j, :, :, pl.ds(pl.multiple_of(n * dgw, 128), dgw)] = partial(j, c, n)

    y_left = lax.rem(y + 3, 4)
    y_right = lax.rem(y + 1, 4)
    y_far = lax.rem(y + 2, 4)

    def pair_sum(j, at):
        return own_p[j, at].astype(F32) + recv_c[j, at].astype(F32)

    def rs_copy(j, n):
        src, dst, to = (
            (st1_s.at[0], st1_r.at[j, 0], right),
            (st1_s.at[1], st1_r.at[j, 1], left),
            (st2_s.at[0], st2_r.at[j, 0], right),
            (st2_s.at[1], st2_r.at[j, 1], left),
        )[n]
        return remote(src, dst, rs_s.at[j, n], rs_r.at[j, n], to)

    def reduce_far(j):
        pair_copy(j).wait_recv()
        if j > 0:
            rs_copy(j - 1, 0).wait_send()
            rs_copy(j - 1, 1).wait_send()
        total = pair_sum(j, y_far)
        st1_s[0] = total[:32].astype(BF16)
        st1_s[1] = total[32:].astype(BF16)
        rs_copy(j, 0).start()
        rs_copy(j, 1).start()

    def reduce_near(j):
        if j > 0:
            rs_copy(j - 1, 2).wait_send()
            rs_copy(j - 1, 3).wait_send()
        rs_copy(j, 0).wait_recv()
        total = pair_sum(j, y_right)
        st2_s[0, :32] = (total[:32] + st1_r[j, 0].astype(F32)).astype(BF16)
        st2_s[0, 32:] = total[32:].astype(BF16)
        rs_copy(j, 2).start()
        rs_copy(j, 1).wait_recv()
        total = pair_sum(j, y_left)
        st2_s[1, :32] = total[:32].astype(BF16)
        st2_s[1, 32:] = (total[32:] + st1_r[j, 1].astype(F32)).astype(BF16)
        rs_copy(j, 3).start()

    def reduce_last(j):
        rs_copy(j, 2).wait_recv()
        rs_copy(j, 3).wait_recv()
        total = pair_sum(j, y) + st2_r[j, 0].astype(F32) + st2_r[j, 1].astype(F32)
        total = total.astype(BF16)
        stacked = jnp.concatenate(
            [total[:, g * dgw : (g + 1) * dgw] for g in range(GROUPS)], axis=0
        )
        a2a_drain(send_g, 0, j)
        send_g[j] = mm(fold_m[...], stacked).astype(BF16).reshape(16, 16, dgw)
        a2a_start(send_g, recv_r, 2, j)

    def own_rows(src, buf, kind, j):
        a2a_wait(src, kind, j)
        unfold(src, buf, j)
        gather_own(buf, kind, j)

    own_rows(recv_g, full_g, 0, 0)
    own_rows(recv_g, full_g, 0, 1)
    make_hidden(0)
    gather_near(full_g, 0, 0)
    own_rows(recv_g, full_g, 0, 2)
    make_hidden(1)
    gather_far(full_g, 0, 0)
    gather_near(full_g, 0, 1)
    make_hidden(2)
    for load in loads[5:]:
        load.wait()
    gather_rest(full_g, 0, 0)
    compute(0)
    gather_near(full_g, 0, 2)
    partials(0)
    gather_far(full_g, 0, 1)
    reduce_far(0)
    own_rows(recv_i, full_i, 1, 0)
    gather_far(full_g, 0, 2)
    gather_rest(full_g, 0, 1)
    compute(1)
    partials(1)
    reduce_far(1)
    reduce_near(0)
    gather_rest(full_g, 0, 2)
    compute(2)
    partials(2)
    reduce_far(2)
    reduce_near(1)
    reduce_last(0)
    gather_near(full_i, 1, 0)
    reduce_near(2)
    own_rows(recv_i, full_i, 1, 1)
    own_rows(recv_i, full_i, 1, 2)

    def transpose_grads(j):
        @pl.loop(0, 2)
        def _(n):
            at = pl.ds(pl.multiple_of(n * 256, 256), 256)
            here = pl.ds(j * 512, 512)
            a_perm[j, at, :] = transposed(ga[here, at])
            b_perm[j, at, :] = transposed(gb[here, at])

    for j in range(CHUNKS):
        transpose_grads(j)

    reduce_last(1)

    tile = 512

    @pl.loop(0, width // tile)
    def _(n):
        at = pl.ds(pl.multiple_of(n * tile, tile), tile)
        total = None
        for j in range(CHUNKS):
            term = mm(hid_t[j], full_g[j, :, :, at].reshape(rows, tile))
            total = term if total is None else total + term
        down[:, at] = total.astype(BF16)

    down_out = pltpu.make_async_copy(down, grad_down_hbm, out_sem.at[0])
    down_out.start()

    gather_far(full_i, 1, 0)
    reduce_last(2)
    gather_near(full_i, 1, 1)

    def bring_back(j):
        a2a_wait(recv_r, 2, j)
        for g in range(GROUPS):
            part = slice(g * dgw, (g + 1) * dgw)
            wanted = cols[0].astype(jnp.int32)
            wanted = jnp.concatenate([wanted, wanted], axis=1) + (4 * g - 256 * j)
            take = (iota((128, 256), 1) == wanted).astype(BF16)
            moved = mm(take, recv_r[j].reshape(256, dgw))
            if j == 0:
                gs[:, part] = moved
            else:
                gs[:, part] += moved

    for j in range(CHUNKS):
        bring_back(j)
    score = cols[2][:, :1]
    grad_score = jnp.zeros((128, 1), F32)
    for g in range(GROUPS):
        part = slice(g * dgw, (g + 1) * dgw)
        grad_score += jnp.sum(tok[:, part].astype(F32) * gs[:, part], axis=1, keepdims=True)
    grad_logit = grad_score * score * (1.0 - score)
    lane_e = iota((128, 16), 1).astype(F32)
    onehot = (lane_e == cols[1][:, :16]).astype(BF16)
    expert_t = iota((16, 128), 0) == routing_ref[...]
    weight_t = jnp.where(expert_t, to_row(grad_logit), 0.0)
    w_high = weight_t.astype(BF16)
    rest = weight_t - w_high.astype(F32)
    w_mid = rest.astype(BF16)
    w_low = (rest - w_mid.astype(F32)).astype(BF16)
    weights3 = jnp.concatenate([w_high, w_mid, w_low], axis=0)
    for g in range(GROUPS):
        part = slice(g * dgw, (g + 1) * dgw)
        share = mm(weights3, tok[:, part])
        share = share[:16] + share[16:32] + share[32:]
        rp_s[g] = share[:8]
        rp_s[4 + g] = share[8:]

    def all_tensor(src, dst, n, whole):
        @pl.loop(1, 8)
        def _(k):
            to = lax.rem(t + k, 8)
            block = src if whole else src.at[to]
            remote(block, dst.at[t], rt_s.at[n], rt_r.at[n], (d, to)).start()

    def wait_tensor(dst, n, sem):
        block = dst.at[pl.ds(0, 7)]
        pltpu.make_async_copy(block, block, sem.at[n]).wait()

    all_tensor(rp_s, rp_r, 0, False)
    rp_r[t] = rp_s[t]

    for g in range(GROUPS):
        part = slice(g * dgw, (g + 1) * dgw)
        picked = mm(onehot, rw[part, :], NT)
        ogr[:, part] = (score * gs[:, part] + grad_logit * picked).astype(BF16)
    tokens_out = pltpu.make_async_copy(ogr, grad_tokens_hbm, out_sem.at[1])
    tokens_out.start()

    wait_tensor(rp_r, 0, rt_r)
    rd_s[...] = jnp.sum(rp_r[...], axis=0)

    @pl.loop(1, 16)
    def _(k):
        to = lax.rem(d + k, 16)
        remote(rd_s, rd_r.at[d], rt_s.at[1], rt_r.at[1], (to, t)).start()

    rd_r[d] = rd_s[...]

    gather_far(full_i, 1, 1)
    gather_near(full_i, 1, 2)

    block = rd_r.at[pl.ds(0, 15)]
    pltpu.make_async_copy(block, block, rt_r.at[1]).wait()
    ro_s[...] = jnp.sum(rd_r[...], axis=0)
    all_tensor(ro_s, ro_r, 2, True)
    ro_r[t] = ro_s[...]
    gather_far(full_i, 1, 2)
    wait_tensor(ro_r, 2, rt_r)
    for g in range(GROUPS):
        part = slice(g * dgw, (g + 1) * dgw)
        grad_router_ref[:8, part] = ro_r[g]
        grad_router_ref[8:, part] = ro_r[4 + g]

    for j in range(CHUNKS):
        gather_rest(full_i, 1, j)

    @pl.loop(0, width // 256)
    def _(n):
        at = pl.ds(pl.multiple_of(n * 256, 256), 256)
        for src, dst, hbm, k in ((a_perm, gate, grad_gate_hbm, 2), (b_perm, up, grad_up_hbm, 3)):
            total = None
            for j in range(CHUNKS):
                term = mm(src[j], full_i[j, :, :, at].reshape(rows, 256))
                total = term if total is None else total + term
            dst[at, :] = transposed(total.astype(BF16))
            pltpu.make_async_copy(dst.at[at, :], hbm.at[at, :], out_sem.at[k]).start()

    down_out.wait()
    tokens_out.wait()
    pltpu.make_async_copy(gate, grad_gate_hbm, out_sem.at[2]).wait()
    pltpu.make_async_copy(up, grad_up_hbm, out_sem.at[3]).wait()
    for j in range(CHUNKS):
        a2a_drain(send_i, 1, j)
        a2a_drain(send_g, 2, j)
        for n in range(8):
            gather_copy(full_g, 0, j, n).wait_send()
            gather_copy(full_i, 1, j, n).wait_send()
    pair_copy(CHUNKS - 1).wait_send()
    for n in range(4):
        rs_copy(CHUNKS - 1, n).wait_send()
    wait_tensor(rp_s, 0, rt_s)
    block = rd_r.at[pl.ds(0, 15)]
    pltpu.make_async_copy(block, block, rt_s.at[1]).wait()
    wait_tensor(ro_r, 2, rt_s)


def local(
    tokens,
    out_grad,
    routing,
    router_weight,
    gate_weight,
    up_weight,
    down_weight,
    saved_gate,
    saved_up,
):
    count, width = tokens.shape
    experts = router_weight.shape[1]
    slots = saved_gate.shape[1]
    hidden = saved_gate.shape[2]
    per = slots // CHUNKS
    dgw = width // GROUPS
    anywhere = pl.BlockSpec(memory_space=pl.ANY)
    vmem = pl.BlockSpec(memory_space=pltpu.VMEM)
    dma = pltpu.SemaphoreType.DMA
    folded = pltpu.VMEM((CHUNKS, experts, 16, dgw), BF16)
    outs = pl.pallas_call(
        kernel,
        out_shape=(
            jax.ShapeDtypeStruct((count, width), BF16),
            jax.ShapeDtypeStruct((width, hidden), BF16),
            jax.ShapeDtypeStruct((width, hidden), BF16),
            jax.ShapeDtypeStruct((hidden, width), BF16),
            jax.ShapeDtypeStruct((experts, width), F32),
        ),
        in_specs=[vmem] + [anywhere] * 8,
        out_specs=(anywhere, anywhere, anywhere, anywhere, vmem),
        scratch_shapes=[
            pltpu.VMEM((count, width), BF16),
            pltpu.VMEM((count, width), BF16),
            pltpu.VMEM((count, width), BF16),
            pltpu.VMEM((width, experts), BF16),
            pltpu.VMEM((width, hidden), BF16),
            pltpu.VMEM((width, hidden), BF16),
            pltpu.VMEM((hidden, width), BF16),
            pltpu.VMEM((CHUNKS, per, hidden), BF16),
            pltpu.VMEM((CHUNKS, per, hidden), BF16),
            pltpu.VMEM((CHUNKS, hidden, per), BF16),
            pltpu.VMEM((slots, hidden), BF16),
            pltpu.VMEM((slots, hidden), BF16),
            folded,
            folded,
            folded,
            folded,
            folded,
            pltpu.VMEM((CHUNKS, 8, 64, width), BF16),
            pltpu.VMEM((CHUNKS, 8, 64, width), BF16),
            pltpu.VMEM((4, 64, width), BF16),
            pltpu.VMEM((CHUNKS, 4, 64, width), BF16),
            pltpu.VMEM((CHUNKS, 4, 64, width), BF16),
            pltpu.VMEM((2, 32, width), BF16),
            pltpu.VMEM((CHUNKS, 2, 32, width), BF16),
            pltpu.VMEM((2, 64, width), BF16),
            pltpu.VMEM((CHUNKS, 2, 64, width), BF16),
            pltpu.VMEM((256, 256), BF16),
            pltpu.VMEM((256, 256), BF16),
            pltpu.VMEM((384, 384), BF16),
            pltpu.VMEM((256, 256), BF16),
            pltpu.VMEM((count, width), F32),
            pltpu.VMEM((1, 128), jnp.int32),
            pltpu.VMEM((3, 128, 128), F32),
            pltpu.VMEM((8, 8, dgw), F32),
            pltpu.VMEM((8, 8, dgw), F32),
            pltpu.VMEM((8, dgw), F32),
            pltpu.VMEM((16, 8, dgw), F32),
            pltpu.VMEM((8, dgw), F32),
            pltpu.VMEM((8, 8, dgw), F32),
            dma((8,)),
            dma((3, CHUNKS)),
            dma((3, CHUNKS)),
            dma((2, CHUNKS, 8)),
            dma((2, CHUNKS, 8)),
            dma((CHUNKS,)),
            dma((CHUNKS,)),
            dma((CHUNKS, 4)),
            dma((CHUNKS, 4)),
            dma((3,)),
            dma((3,)),
            dma((4,)),
        ],
        compiler_params=pltpu.CompilerParams(
            collective_id=0, has_side_effects=True, vmem_limit_bytes=63 * 2**20
        ),
        cost_estimate=pl.CostEstimate(
            flops=12 * slots * width * hidden,
            bytes_accessed=2 * (6 * width * hidden + 2 * slots * hidden + 4 * count * width),
            transcendentals=slots * hidden,
        ),
    )(
        routing.reshape(1, count),
        tokens,
        out_grad,
        router_weight,
        gate_weight[0],
        up_weight[0],
        down_weight[0],
        saved_gate[0],
        saved_up[0],
    )
    grad_tokens, grad_gate, grad_up, grad_down, grad_router = outs
    return grad_tokens, grad_gate[None], grad_up[None], grad_down[None], grad_router.T


def solution(mesh):
    placed = (
        P(("dp", "tensor"), None),
        P(("dp", "tensor"), None),
        P(("dp", "tensor"), None),
        P(),
        P("dp", None, "tensor"),
        P("dp", None, "tensor"),
        P("dp", "tensor", None),
        P("dp", None, "tensor"),
        P("dp", None, "tensor"),
    )
    return jax.shard_map(
        local,
        mesh=mesh,
        in_specs=placed,
        out_specs=(
            P(("dp", "tensor"), None),
            P("dp", None, "tensor"),
            P("dp", None, "tensor"),
            P("dp", "tensor", None),
            P(),
        ),
        check_vma=False,
    )
```

```python
import jax
import jax.numpy as jnp
from jax import lax
from jax.experimental import pallas as pl
from jax.experimental.pallas import tpu as pltpu
from jax.sharding import PartitionSpec as P

MESH = pl.DeviceIdType.MESH
NN = (((1,), (0,)), ((), ()))
NT = (((1,), (1,)), ((), ()))
TN = (((0,), (0,)), ((), ()))
F32 = jnp.float32
BF16 = jnp.bfloat16

CHUNKS = 3
GROUPS = 4


def mm(a, b, dims=NN):
    return lax.dot_general(a, b, dims, preferred_element_type=F32)


def iota(shape, dim):
    return lax.broadcasted_iota(jnp.int32, shape, dim)


def eye_mask(n):
    return iota((n, n), 0) == iota((n, n), 1)


def kernel(
    routing_ref,
    tokens_hbm,
    out_grad_hbm,
    router_hbm,
    gate_hbm,
    up_hbm,
    down_hbm,
    saved_gate_hbm,
    saved_up_hbm,
    grad_tokens_hbm,
    early_hbm,
    late_in_hbm,
    late_grad_hbm,
    grad_down_hbm,
    grad_router_ref,
    tok,
    ogr,
    tok_rows,
    row_score,
    rw,
    weights,
    down,
    a_perm,
    b_perm,
    hid_t,
    gab,
    send_g,
    send_i,
    recv_g,
    recv_i,
    recv_r,
    full_g,
    full_i,
    send_c,
    own_p,
    recv_c,
    st1_s,
    st1_r,
    st2_s,
    st2_r,
    unfold_m,
    fold_m,
    save_m,
    gs,
    tgt_row,
    cols,
    rx_s,
    rx_r,
    ry_s,
    ry_r,
    load_sem,
    a2a_s,
    a2a_r,
    ag_s,
    ag_r,
    pc_s,
    pc_r,
    rs_s,
    rs_r,
    rt_s,
    rt_r,
    out_sem,
):
    d = lax.axis_index("dp")
    t = lax.axis_index("tensor")
    y = t // 2
    c = lax.rem(t, 2)
    right = (d, lax.rem(y + 1, 4) * 2 + c)
    left = (d, lax.rem(y + 3, 4) * 2 + c)
    partner = (d, y * 2 + 1 - c)
    mine = c * 4 + y
    from_left = c * 4 + lax.rem(y + 3, 4)
    from_right = c * 4 + lax.rem(y + 1, 4)
    far = c * 4 + lax.rem(y + 2, 4)
    dgw = tok.shape[1] // GROUPS
    rows = full_g.shape[1] * full_g.shape[2]
    width = tok.shape[1]
    hidden = down.shape[0]

    loads = [
        pltpu.make_async_copy(src, dst, load_sem.at[n])
        for n, (src, dst) in enumerate(
            (
                (out_grad_hbm, ogr),
                (tokens_hbm, tok),
                (router_hbm, rw),
                (saved_gate_hbm, gab.at[:, pl.ds(0, hidden)]),
                (saved_up_hbm, gab.at[:, pl.ds(hidden, hidden)]),
                (down_hbm, down),
                (gate_hbm, weights.at[:, pl.ds(0, hidden)]),
                (up_hbm, weights.at[:, pl.ds(hidden, hidden)]),
            )
        )
    ]
    for load in loads[:3]:
        load.start()

    barrier = pltpu.get_barrier_semaphore()

    @pl.loop(1, 16)
    def _(k):
        pl.semaphore_signal(
            barrier, inc=1, device_id=(lax.rem(d + k, 16), t), device_id_type=MESH
        )

    @pl.loop(1, 8)
    def _(k):
        pl.semaphore_signal(
            barrier, inc=1, device_id=(d, lax.rem(t + k, 8)), device_id_type=MESH
        )

    def remote(src, dst, send_sem, recv_sem, to):
        return pltpu.make_async_remote_copy(
            src_ref=src,
            dst_ref=dst,
            send_sem=send_sem,
            recv_sem=recv_sem,
            device_id=to,
            device_id_type=MESH,
        )

    def a2a_start(src, dst, kind, j):
        @pl.loop(1, 16)
        def _(k):
            to = lax.rem(d + k, 16)
            remote(
                src.at[j, to], dst.at[j, d], a2a_s.at[kind, j], a2a_r.at[kind, j], (to, t)
            ).start()

        dst[j, d] = src[j, d]

    def a2a_wait(dst, kind, j):
        part = dst.at[j, pl.ds(0, 15)]
        pltpu.make_async_copy(part, part, a2a_r.at[kind, j]).wait()

    def a2a_drain(src, kind, j):
        part = src.at[j, pl.ds(0, 15)]
        pltpu.make_async_copy(part, part, a2a_s.at[kind, j]).wait()

    def gather_copy(buf, kind, j, n):
        block, to = (
            (buf.at[j, mine], right),
            (buf.at[j, mine], left),
            (buf.at[j, from_left, pl.ds(0, 32)], right),
            (buf.at[j, from_right, pl.ds(32, 32)], left),
            (buf.at[j, mine], partner),
            (buf.at[j, from_left], partner),
            (buf.at[j, from_right], partner),
            (buf.at[j, far], partner),
        )[n]
        return remote(block, block, ag_s.at[kind, j, n], ag_r.at[kind, j, n], to)

    def gather_own(buf, kind, j):
        for n in (0, 1, 4):
            gather_copy(buf, kind, j, n).start()

    def landed(buf, kind, j, n):
        other = (1 - c) * 4
        block = (
            lambda: buf.at[j, from_left],
            lambda: buf.at[j, from_right],
            lambda: buf.at[j, far, pl.ds(0, 32)],
            lambda: buf.at[j, far, pl.ds(32, 32)],
            lambda: buf.at[j, other + y],
            lambda: buf.at[j, other + lax.rem(y + 3, 4)],
            lambda: buf.at[j, other + lax.rem(y + 1, 4)],
            lambda: buf.at[j, other + lax.rem(y + 2, 4)],
        )[n]()
        remote(block, block, ag_s.at[kind, j, n], ag_r.at[kind, j, n], partner).wait_recv()

    def gather_near(buf, kind, j):
        landed(buf, kind, j, 0)
        gather_copy(buf, kind, j, 2).start()
        gather_copy(buf, kind, j, 5).start()
        landed(buf, kind, j, 1)
        gather_copy(buf, kind, j, 3).start()
        gather_copy(buf, kind, j, 6).start()

    def gather_far(buf, kind, j):
        landed(buf, kind, j, 2)
        landed(buf, kind, j, 3)
        gather_copy(buf, kind, j, 7).start()

    def gather_rest(buf, kind, j):
        for n in (4, 5, 6, 7):
            landed(buf, kind, j, n)

    e_row = routing_ref[...]
    expert_t = iota((16, 128), 0) == e_row
    onehot_t = expert_t.astype(F32)
    before = (iota((128, 128), 0) < iota((128, 128), 1)).astype(BF16)
    earlier = mm(onehot_t.astype(BF16), before)
    slot = jnp.sum(earlier * onehot_t, axis=0, keepdims=True)
    high = (slot >= 4.0).astype(F32) + (slot >= 8.0).astype(F32)
    e_float = e_row.astype(F32)
    target = high * 252.0 + e_float * 16.0 + slot
    tgt_row[...] = target.astype(jnp.int32)
    eye128 = eye_mask(128)

    def to_column(row):
        return jnp.sum(jnp.where(eye128, row, 0.0), axis=1, keepdims=True)

    def to_row(column):
        return jnp.sum(jnp.where(eye128, column, 0.0), axis=0, keepdims=True)

    cols[0] = jnp.broadcast_to(to_column(target), (128, 128))
    cols[1] = jnp.broadcast_to(to_column(e_float), (128, 128))

    def fold_tokens(src, dst, j):
        total = None
        for g in range(GROUPS):
            place = (iota((256, 128), 0) == tgt_row[...] + (4 * g - 256 * j)).astype(BF16)
            term = mm(place, src[:, g * dgw : (g + 1) * dgw])
            total = term if total is None else total + term
        dst[j] = total.astype(BF16).reshape(16, 16, dgw)

    out_at = iota((256, 256), 0)
    in_at = iota((256, 256), 1)
    unfold_m[...] = (
        in_at == ((out_at >> 2) & 15) * 16 + (out_at >> 6) * 4 + (out_at & 3)
    ).astype(BF16)
    fold_m[...] = (
        in_at == ((out_at >> 2) & 3) * 64 + (out_at >> 4) * 4 + (out_at & 3)
    ).astype(BF16)

    save_out = iota((384, 384), 0)
    save_m[...] = (
        iota((384, 384), 1)
        == ((save_out >> 2) & 3) * 96
        + (((save_out >> 4) & 3) * 2 + ((save_out >> 6) & 1)) * 12
        + (save_out >> 7) * 4
        + (save_out & 3)
    ).astype(BF16)
    def permute_saved(start, dst):
        @pl.loop(0, 4)
        def _(q):
            block = gab[pl.ds(pl.multiple_of(q * 384, 384), 384), start : start + hidden]
            moved = mm(save_m[...], block).astype(BF16)
            for j in range(CHUNKS):
                for p in range(8):
                    first = (j * 8 + p) * 16
                    dst[j, pl.ds(pl.multiple_of(p * 64 + q * 16, 16), 16), :] = moved[
                        first : first + 16, :
                    ]

    def unfold(src, buf, j):
        moved = mm(unfold_m[...], src[j].reshape(256, dgw)).astype(BF16)
        for g in range(GROUPS):
            buf[j, mine, :, g * dgw : (g + 1) * dgw] = moved[g * 64 : (g + 1) * 64, :]

    def make_hidden(j):
        @pl.loop(0, hidden // 256)
        def _(n):
            at = pl.ds(pl.multiple_of(n * 256, 256), 256)
            a = a_perm[j, :, at].astype(F32)
            b = b_perm[j, :, at].astype(F32)
            value = (a * jax.nn.sigmoid(a) * b).astype(BF16)
            hid_t[at, j * rows : (j + 1) * rows] = value.T

    def compute(j):
        @pl.loop(0, hidden // 256)
        def _(n):
            at = pl.ds(pl.multiple_of(n * 256, 256), 256)
            too = pl.ds(pl.multiple_of(n * 256 + hidden, 256), 256)
            gh = mm(full_g[j].reshape(rows, width), down[at, :], NT)
            a = a_perm[j, :, at].astype(F32)
            b = b_perm[j, :, at].astype(F32)
            sg = jax.nn.sigmoid(a)
            silu = a * sg
            here = pl.ds(j * rows, rows)
            gab[here, at] = (gh * b * sg * (1.0 + a * (1.0 - sg))).astype(BF16)
            gab[here, too] = (gh * silu).astype(BF16)

    def partial(j, parity, n):
        at = pl.ds(pl.multiple_of(j * rows + parity * 256, 256), 256)
        hold = pl.ds(pl.multiple_of(n * dgw, 128), dgw)
        return mm(gab[at, :], weights[hold, :], NT).astype(BF16).reshape(4, 64, dgw)

    def pair_copy(j):
        return remote(send_c, recv_c.at[j], pc_s.at[j], pc_r.at[j], partner)

    def partials(j):
        if j > 0:
            pair_copy(j - 1).wait_send()

        @pl.loop(0, GROUPS)
        def _(n):
            send_c[:, :, pl.ds(pl.multiple_of(n * dgw, 128), dgw)] = partial(j, 1 - c, n)

        pair_copy(j).start()

        @pl.loop(0, GROUPS)
        def _(n):
            own_p[j, :, :, pl.ds(pl.multiple_of(n * dgw, 128), dgw)] = partial(j, c, n)

    y_left = lax.rem(y + 3, 4)
    y_right = lax.rem(y + 1, 4)
    y_far = lax.rem(y + 2, 4)

    def pair_sum(j, at):
        return own_p[j, at].astype(F32) + recv_c[j, at].astype(F32)

    def rs_copy(j, n):
        src, dst, to = (
            (st1_s.at[0], st1_r.at[j, 0], right),
            (st1_s.at[1], st1_r.at[j, 1], left),
            (st2_s.at[0], st2_r.at[j, 0], right),
            (st2_s.at[1], st2_r.at[j, 1], left),
        )[n]
        return remote(src, dst, rs_s.at[j, n], rs_r.at[j, n], to)

    def reduce_far(j):
        pair_copy(j).wait_recv()
        if j > 0:
            rs_copy(j - 1, 0).wait_send()
            rs_copy(j - 1, 1).wait_send()
        total = pair_sum(j, y_far)
        st1_s[0] = total[:32].astype(BF16)
        st1_s[1] = total[32:].astype(BF16)
        rs_copy(j, 0).start()
        rs_copy(j, 1).start()

    def reduce_near(j):
        if j > 0:
            rs_copy(j - 1, 2).wait_send()
            rs_copy(j - 1, 3).wait_send()
        rs_copy(j, 0).wait_recv()
        total = pair_sum(j, y_right)
        st2_s[0, :32] = (total[:32] + st1_r[j, 0].astype(F32)).astype(BF16)
        st2_s[0, 32:] = total[32:].astype(BF16)
        rs_copy(j, 2).start()
        rs_copy(j, 1).wait_recv()
        total = pair_sum(j, y_left)
        st2_s[1, :32] = total[:32].astype(BF16)
        st2_s[1, 32:] = (total[32:] + st1_r[j, 1].astype(F32)).astype(BF16)
        rs_copy(j, 3).start()

    def reduce_last(j):
        rs_copy(j, 2).wait_recv()
        rs_copy(j, 3).wait_recv()
        total = pair_sum(j, y) + st2_r[j, 0].astype(F32) + st2_r[j, 1].astype(F32)
        total = total.astype(BF16)
        token = tok_rows[j].astype(F32)
        score = row_score[j][:, :1]
        grad_score = jnp.sum(token * total.astype(F32), axis=1, keepdims=True)
        grad_logit = grad_score * score * (1.0 - score)
        share = jnp.sum(token * grad_logit, axis=0, keepdims=True)
        if j == 0:
            rx_s[...] = share
        else:
            rx_s[...] += share
        stacked = jnp.concatenate(
            [total[:, g * dgw : (g + 1) * dgw] for g in range(GROUPS)], axis=0
        )
        a2a_drain(send_g, 0, j)
        send_g[j] = mm(fold_m[...], stacked).astype(BF16).reshape(16, 16, dgw)
        a2a_start(send_g, recv_r, 2, j)

    def own_grads(j):
        a2a_wait(recv_g, 0, j)
        moved = mm(unfold_m[...], recv_g[j].reshape(256, dgw)).astype(BF16)
        for g in range(GROUPS):
            full_g[j, mine, :, g * dgw : (g + 1) * dgw] = moved[g * 64 : (g + 1) * 64, :]
        gather_own(full_g, 0, j)

    def own_inputs(j):
        a2a_wait(recv_i, 1, j)
        moved = mm(unfold_m[...], recv_i[j].reshape(256, dgw)).astype(BF16)
        for g in range(GROUPS):
            tok_rows[j, :, g * dgw : (g + 1) * dgw] = moved[g * 64 : (g + 1) * 64, :]
        logits = mm(tok_rows[j], rw[...], NT)
        logit = jnp.sum(jnp.where(iota((64, 16), 1) == d, logits, 0.0), axis=1, keepdims=True)
        score = jax.nn.sigmoid(logit)
        row_score[j] = jnp.broadcast_to(score, (64, 128))
        full_i[j, mine] = (score * tok_rows[j].astype(F32)).astype(BF16)

    loads[0].wait()
    for j in range(CHUNKS):
        fold_tokens(ogr, send_g, j)
        if j == 0:
            pl.semaphore_wait(barrier, 22)
        a2a_start(send_g, recv_g, 0, j)
    for load in loads[3:]:
        load.start()
    loads[1].wait()
    for j in range(CHUNKS):
        own_grads(j)
        fold_tokens(tok, send_i, j)
        a2a_start(send_i, recv_i, 1, j)
    gather_near(full_g, 0, 0)
    loads[3].wait()
    loads[4].wait()
    permute_saved(0, a_perm)
    gather_near(full_g, 0, 1)
    permute_saved(hidden, b_perm)
    gather_far(full_g, 0, 0)
    for load in loads[5:]:
        load.wait()
    loads[2].wait()
    own_inputs(0)
    gather_near(full_g, 0, 2)
    gather_own(full_i, 1, 0)
    gather_rest(full_g, 0, 0)
    compute(0)
    gather_far(full_g, 0, 1)
    partials(0)
    gather_far(full_g, 0, 2)
    reduce_far(0)
    gather_rest(full_g, 0, 1)
    compute(1)
    partials(1)
    reduce_near(0)
    reduce_far(1)
    gather_rest(full_g, 0, 2)
    compute(2)
    gather_near(full_i, 1, 0)
    partials(2)
    reduce_near(1)
    reduce_far(2)
    own_inputs(1)
    gather_own(full_i, 1, 1)
    reduce_last(0)
    own_inputs(2)
    late_grad = pltpu.make_async_copy(
        gab.at[pl.ds(2 * rows, rows)], late_grad_hbm, out_sem.at[4]
    )
    late_grad.start()
    make_hidden(0)
    make_hidden(1)
    make_hidden(2)
    logits = mm(tok[...], rw[...], NT)
    lane_e = iota((128, 16), 1).astype(F32)
    onehot = (lane_e == cols[1][:, :16]).astype(F32)
    score = jax.nn.sigmoid(jnp.sum(logits * onehot, axis=1, keepdims=True))
    cols[2] = jnp.broadcast_to(score, (128, 128))
    reduce_near(2)
    gather_far(full_i, 1, 0)

    tile = 512

    @pl.loop(0, width // tile)
    def _(n):
        at = pl.ds(pl.multiple_of(n * tile, tile), tile)
        down[:, at] = mm(hid_t[...], full_g[:, :, :, at].reshape(CHUNKS * rows, tile)).astype(BF16)

    down_out = pltpu.make_async_copy(down, grad_down_hbm, out_sem.at[0])
    down_out.start()
    reduce_last(1)
    gather_near(full_i, 1, 1)
    gather_own(full_i, 1, 2)
    reduce_last(2)

    @pl.loop(1, 8)
    def _(k):
        to = lax.rem(t + k, 8)
        remote(rx_s, rx_r.at[t], rt_s.at[0], rt_r.at[0], (d, to)).start()

    rx_r[t] = rx_s[...]

    def bring_back(j):
        a2a_wait(recv_r, 2, j)
        for g in range(GROUPS):
            part = slice(g * dgw, (g + 1) * dgw)
            wanted = cols[0].astype(jnp.int32)
            wanted = jnp.concatenate([wanted, wanted], axis=1) + (4 * g - 256 * j)
            take = (iota((128, 256), 1) == wanted).astype(BF16)
            moved = mm(take, recv_r[j].reshape(256, dgw))
            if j == 0:
                gs[:, part] = moved
            else:
                gs[:, part] += moved

    bring_back(0)
    bring_back(1)
    gather_far(full_i, 1, 1)
    bring_back(2)
    score = cols[2][:, :1]
    grad_score = jnp.zeros((128, 1), F32)
    for g in range(GROUPS):
        part = slice(g * dgw, (g + 1) * dgw)
        grad_score += jnp.sum(tok[:, part].astype(F32) * gs[:, part], axis=1, keepdims=True)
    grad_logit = grad_score * score * (1.0 - score)
    lane_e = iota((128, 16), 1).astype(F32)
    onehot = (lane_e == cols[1][:, :16]).astype(BF16)
    for g in range(GROUPS):
        part = slice(g * dgw, (g + 1) * dgw)
        picked = mm(onehot, rw[:, part])
        ogr[:, part] = (score * gs[:, part] + grad_logit * picked).astype(BF16)
    tokens_out = pltpu.make_async_copy(ogr, grad_tokens_hbm, out_sem.at[1])
    tokens_out.start()

    block = rx_r.at[pl.ds(0, 7)]
    pltpu.make_async_copy(block, block, rt_r.at[0]).wait()
    ry_s[...] = jnp.sum(rx_r[...], axis=0)

    @pl.loop(1, 16)
    def _(k):
        to = lax.rem(d + k, 16)
        remote(ry_s, ry_r.at[d], rt_s.at[1], rt_r.at[1], (to, t)).start()

    ry_r[d] = ry_s[...]

    def early(first, last):
        @pl.loop(first, last)
        def _(n):
            at = pl.ds(pl.multiple_of(n * 256, 256), 256)
            value = mm(full_i[:2, :, :, at].reshape(2 * rows, 256), gab[: 2 * rows, :], TN)
            weights[at, :] = value.astype(BF16)
            pltpu.make_async_copy(
                weights.at[at, :], early_hbm.at[at, :], out_sem.at[2]
            ).start()

    def late_in(p):
        pltpu.make_async_copy(full_i.at[2, p], late_in_hbm.at[p], out_sem.at[3]).start()

    steps = width // 256
    gather_near(full_i, 1, 2)
    gather_rest(full_i, 1, 0)
    gather_rest(full_i, 1, 1)
    early(0, steps // 2)
    gather_far(full_i, 1, 2)
    early(steps // 2, steps)
    block = ry_r.at[pl.ds(0, 15)]
    pltpu.make_async_copy(block, block, rt_r.at[1]).wait()
    for k in range(16):
        grad_router_ref[k : k + 1, :] = ry_r[k]
    gather_rest(full_i, 1, 2)
    for p in range(8):
        late_in(p)

    down_out.wait()
    tokens_out.wait()
    late_grad.wait()
    pltpu.make_async_copy(weights, early_hbm, out_sem.at[2]).wait()
    pltpu.make_async_copy(full_i.at[2], late_in_hbm, out_sem.at[3]).wait()
    for j in range(CHUNKS):
        a2a_drain(send_i, 1, j)
        a2a_drain(send_g, 2, j)
        for n in range(8):
            gather_copy(full_g, 0, j, n).wait_send()
            gather_copy(full_i, 1, j, n).wait_send()
    pair_copy(CHUNKS - 1).wait_send()
    for n in range(4):
        rs_copy(CHUNKS - 1, n).wait_send()
    block = rx_r.at[pl.ds(0, 7)]
    pltpu.make_async_copy(block, block, rt_s.at[0]).wait()
    block = ry_r.at[pl.ds(0, 15)]
    pltpu.make_async_copy(block, block, rt_s.at[1]).wait()


def finish(
    early_hbm,
    late_in_hbm,
    late_grad_hbm,
    tokens_in,
    down_in,
    router_in,
    gate_hbm,
    up_hbm,
    tokens_hbm,
    down_hbm,
    router_hbm,
    early,
    late_in,
    late_grad,
    tokens,
    down,
    router,
    gate,
    up,
    in_sem,
    out_sem,
):
    width, hidden = gate.shape
    parts = 5
    step = width // parts
    stripes = [pl.ds(n * step, step) for n in range(parts)]
    moves = [(late_grad_hbm, late_grad), (late_in_hbm, late_in)]
    moves += [(early_hbm.at[at], early.at[at]) for at in stripes]
    moves += [(down_in, down), (tokens_in, tokens), (router_in, router)]
    loads = [pltpu.make_async_copy(a, b, in_sem.at[n]) for n, (a, b) in enumerate(moves)]
    for load in loads:
        load.start()
    stores = []

    def store(src, dst):
        stores.append(pltpu.make_async_copy(src, dst, out_sem.at[len(stores)]))
        stores[-1].start()

    loads[0].wait()
    loads[1].wait()
    for n, at in enumerate(stripes):
        loads[2 + n].wait()
        value = mm(late_in[:, n * step : (n + 1) * step], late_grad[...], TN)
        value = value + early[at, :].astype(F32)
        gate[at, :] = value[:, :hidden].astype(BF16)
        up[at, :] = value[:, hidden:].astype(BF16)
        store(gate.at[at], gate_hbm.at[at])
        store(up.at[at], up_hbm.at[at])
    for n, (src, dst) in enumerate(
        ((down, down_hbm), (tokens, tokens_hbm), (router, router_hbm))
    ):
        loads[2 + parts + n].wait()
        store(src, dst)
    for one in stores:
        one.wait()


def local(
    tokens,
    out_grad,
    routing,
    router_weight,
    gate_weight,
    up_weight,
    down_weight,
    saved_gate,
    saved_up,
):
    count, width = tokens.shape
    experts = router_weight.shape[1]
    slots = saved_gate.shape[1]
    hidden = saved_gate.shape[2]
    per = slots // CHUNKS
    dgw = width // GROUPS
    anywhere = pl.BlockSpec(memory_space=pl.ANY)
    vmem = pl.BlockSpec(memory_space=pltpu.VMEM)
    dma = pltpu.SemaphoreType.DMA
    folded = pltpu.VMEM((CHUNKS, experts, 16, dgw), BF16)
    outs = pl.pallas_call(
        kernel,
        out_shape=(
            jax.ShapeDtypeStruct((count, width), BF16),
            jax.ShapeDtypeStruct((width, 2 * hidden), BF16),
            jax.ShapeDtypeStruct((8, 64, width), BF16),
            jax.ShapeDtypeStruct((per, 2 * hidden), BF16),
            jax.ShapeDtypeStruct((hidden, width), BF16),
            jax.ShapeDtypeStruct((experts, width), F32),
        ),
        in_specs=[vmem] + [anywhere] * 8,
        out_specs=(anywhere, anywhere, anywhere, anywhere, anywhere, vmem),
        scratch_shapes=[
            pltpu.VMEM((count, width), BF16),
            pltpu.VMEM((count, width), BF16),
            pltpu.VMEM((CHUNKS, 64, width), BF16),
            pltpu.VMEM((CHUNKS, 64, 128), F32),
            pltpu.VMEM((experts, width), BF16),
            pltpu.VMEM((width, 2 * hidden), BF16),
            pltpu.VMEM((hidden, width), BF16),
            pltpu.VMEM((CHUNKS, per, hidden), BF16),
            pltpu.VMEM((CHUNKS, per, hidden), BF16),
            pltpu.VMEM((hidden, slots), BF16),
            pltpu.VMEM((slots, 2 * hidden), BF16),
            folded,
            folded,
            folded,
            folded,
            folded,
            pltpu.VMEM((CHUNKS, 8, 64, width), BF16),
            pltpu.VMEM((CHUNKS, 8, 64, width), BF16),
            pltpu.VMEM((4, 64, width), BF16),
            pltpu.VMEM((CHUNKS, 4, 64, width), BF16),
            pltpu.VMEM((CHUNKS, 4, 64, width), BF16),
            pltpu.VMEM((2, 32, width), BF16),
            pltpu.VMEM((CHUNKS, 2, 32, width), BF16),
            pltpu.VMEM((2, 64, width), BF16),
            pltpu.VMEM((CHUNKS, 2, 64, width), BF16),
            pltpu.VMEM((256, 256), BF16),
            pltpu.VMEM((256, 256), BF16),
            pltpu.VMEM((384, 384), BF16),
            pltpu.VMEM((count, width), F32),
            pltpu.VMEM((1, 128), jnp.int32),
            pltpu.VMEM((3, 128, 128), F32),
            pltpu.VMEM((1, width), F32),
            pltpu.VMEM((8, 1, width), F32),
            pltpu.VMEM((1, width), F32),
            pltpu.VMEM((16, 1, width), F32),
            dma((8,)),
            dma((3, CHUNKS)),
            dma((3, CHUNKS)),
            dma((2, CHUNKS, 8)),
            dma((2, CHUNKS, 8)),
            dma((CHUNKS,)),
            dma((CHUNKS,)),
            dma((CHUNKS, 4)),
            dma((CHUNKS, 4)),
            dma((2,)),
            dma((2,)),
            dma((5,)),
        ],
        compiler_params=pltpu.CompilerParams(
            collective_id=0, has_side_effects=True, vmem_limit_bytes=63 * 2**20
        ),
        cost_estimate=pl.CostEstimate(
            flops=12 * slots * width * hidden,
            bytes_accessed=2 * (6 * width * hidden + 2 * slots * hidden + 4 * count * width),
            transcendentals=slots * hidden,
        ),
    )(
        routing.reshape(1, count),
        tokens,
        out_grad,
        router_weight.T,
        gate_weight[0],
        up_weight[0],
        down_weight[0],
        saved_gate[0],
        saved_up[0],
    )
    grad_tokens, early, late_in, late_grad, grad_down, grad_router = outs
    grad_gate, grad_up, grad_tokens, grad_down, grad_router = pl.pallas_call(
        finish,
        out_shape=(
            jax.ShapeDtypeStruct((width, hidden), BF16),
            jax.ShapeDtypeStruct((width, hidden), BF16),
            jax.ShapeDtypeStruct((count, width), BF16),
            jax.ShapeDtypeStruct((hidden, width), BF16),
            jax.ShapeDtypeStruct((experts, width), F32),
        ),
        in_specs=[anywhere] * 6,
        out_specs=(anywhere,) * 5,
        scratch_shapes=[
            pltpu.VMEM((width, 2 * hidden), BF16),
            pltpu.VMEM((per, width), BF16),
            pltpu.VMEM((per, 2 * hidden), BF16),
            pltpu.VMEM((count, width), BF16),
            pltpu.VMEM((hidden, width), BF16),
            pltpu.VMEM((experts, width), F32),
            pltpu.VMEM((width, hidden), BF16),
            pltpu.VMEM((width, hidden), BF16),
            dma((10,)),
            dma((13,)),
        ],
        compiler_params=pltpu.CompilerParams(vmem_limit_bytes=62 * 2**20),
    )(early, late_in.reshape(per, width), late_grad, grad_tokens, grad_down, grad_router)
    return grad_tokens, grad_gate[None], grad_up[None], grad_down[None], grad_router.T


def solution(mesh):
    placed = (
        P(("dp", "tensor"), None),
        P(("dp", "tensor"), None),
        P(("dp", "tensor"), None),
        P(),
        P("dp", None, "tensor"),
        P("dp", None, "tensor"),
        P("dp", "tensor", None),
        P("dp", None, "tensor"),
        P("dp", None, "tensor"),
    )
    return jax.shard_map(
        local,
        mesh=mesh,
        in_specs=placed,
        out_specs=(
            P(("dp", "tensor"), None),
            P("dp", None, "tensor"),
            P("dp", None, "tensor"),
            P("dp", "tensor", None),
            P(),
        ),
        check_vma=False,
    )
```

```python
import jax
import jax.numpy as jnp
from jax import lax
from jax.experimental import pallas as pl
from jax.experimental.pallas import tpu as pltpu
from jax.sharding import PartitionSpec as P

MESH = pl.DeviceIdType.MESH
NN = (((1,), (0,)), ((), ()))
NT = (((1,), (1,)), ((), ()))
TN = (((0,), (0,)), ((), ()))
F32 = jnp.float32
BF16 = jnp.bfloat16

CHUNKS = 3
GROUPS = 4
CROSSED = 1


def mm(a, b, dims=NN):
    return lax.dot_general(a, b, dims, preferred_element_type=F32)


def iota(shape, dim):
    return lax.broadcasted_iota(jnp.int32, shape, dim)


def eye_mask(n):
    return iota((n, n), 0) == iota((n, n), 1)


def kernel(
    routing_ref,
    tokens_hbm,
    out_grad_hbm,
    router_hbm,
    gate_hbm,
    up_hbm,
    down_hbm,
    saved_gate_hbm,
    saved_up_hbm,
    grad_tokens_hbm,
    early_hbm,
    late_in_hbm,
    late_grad_hbm,
    grad_down_hbm,
    grad_router_ref,
    tok,
    ogr,
    tok_rows,
    row_score,
    rw,
    weights,
    down,
    a_perm,
    b_perm,
    hid_t,
    gab,
    send_g,
    send_i,
    recv_g,
    recv_i,
    recv_r,
    full_g,
    full_i,
    send_c,
    own_p,
    recv_c,
    st1_s,
    st1_r,
    st2_s,
    st2_r,
    unfold_m,
    fold_m,
    save_m,
    gs,
    crossed,
    send_a,
    recv_a,
    tgt_row,
    cols,
    rx_s,
    rx_r,
    ry_s,
    ry_r,
    load_sem,
    a2a_s,
    a2a_r,
    cr_s,
    cr_r,
    ca_s,
    ca_r,
    ag_s,
    ag_r,
    pc_s,
    pc_r,
    rs_s,
    rs_r,
    rt_s,
    rt_r,
    out_sem,
):
    d = lax.axis_index("dp")
    t = lax.axis_index("tensor")
    y = t // 2
    c = lax.rem(t, 2)
    right = (d, lax.rem(y + 1, 4) * 2 + c)
    left = (d, lax.rem(y + 3, 4) * 2 + c)
    partner = (d, y * 2 + 1 - c)
    mine = c * 4 + y
    from_left = c * 4 + lax.rem(y + 3, 4)
    from_right = c * 4 + lax.rem(y + 1, 4)
    far = c * 4 + lax.rem(y + 2, 4)
    dgw = tok.shape[1] // GROUPS
    rows = full_g.shape[1] * full_g.shape[2]
    width = tok.shape[1]
    hidden = down.shape[0]
    cut = CROSSED * dgw

    loads = [
        pltpu.make_async_copy(src, dst, load_sem.at[n])
        for n, (src, dst) in enumerate(
            (
                (out_grad_hbm, ogr),
                (tokens_hbm, tok),
                (router_hbm, rw),
                (saved_gate_hbm, gab.at[:, pl.ds(0, hidden)]),
                (saved_up_hbm, gab.at[:, pl.ds(hidden, hidden)]),
                (down_hbm, down),
                (gate_hbm, weights.at[:, pl.ds(0, hidden)]),
                (up_hbm, weights.at[:, pl.ds(hidden, hidden)]),
            )
        )
    ]
    for load in loads[:3]:
        load.start()

    barrier = pltpu.get_barrier_semaphore()

    @pl.loop(1, 16)
    def _(k):
        pl.semaphore_signal(
            barrier, inc=1, device_id=(lax.rem(d + k, 16), t), device_id_type=MESH
        )

    @pl.loop(1, 8)
    def _(k):
        pl.semaphore_signal(
            barrier, inc=1, device_id=(d, lax.rem(t + k, 8)), device_id_type=MESH
        )

    def remote(src, dst, send_sem, recv_sem, to):
        return pltpu.make_async_remote_copy(
            src_ref=src,
            dst_ref=dst,
            send_sem=send_sem,
            recv_sem=recv_sem,
            device_id=to,
            device_id_type=MESH,
        )

    def a2a_start(src, dst, kind, j):
        @pl.loop(1, 16)
        def _(k):
            to = lax.rem(d + k, 16)
            remote(
                src.at[j, to], dst.at[j, d], a2a_s.at[kind, j], a2a_r.at[kind, j], (to, t)
            ).start()

        dst[j, d] = src[j, d]

    def a2a_wait(dst, kind, j):
        part = dst.at[j, pl.ds(0, 15)]
        pltpu.make_async_copy(part, part, a2a_r.at[kind, j]).wait()

    def a2a_drain(src, kind, j):
        part = src.at[j, pl.ds(0, 15)]
        pltpu.make_async_copy(part, part, a2a_s.at[kind, j]).wait()

    def piece(buf, kind, j, p, first=0, count=64):
        if kind == 0:
            return buf.at[j, p, pl.ds(first, count)]
        return buf.at[j, p, pl.ds(first, count), pl.ds(cut, width - cut)]

    def gather_copy(buf, kind, j, n):
        block, to = (
            (piece(buf, kind, j, mine), right),
            (piece(buf, kind, j, mine), left),
            (piece(buf, kind, j, from_left, 0, 32), right),
            (piece(buf, kind, j, from_right, 32, 32), left),
            (piece(buf, kind, j, mine), partner),
            (piece(buf, kind, j, from_left), partner),
            (piece(buf, kind, j, from_right), partner),
            (piece(buf, kind, j, far), partner),
        )[n]
        return remote(block, block, ag_s.at[kind, j, n], ag_r.at[kind, j, n], to)

    def gather_own(buf, kind, j):
        for n in (0, 1, 4):
            gather_copy(buf, kind, j, n).start()

    def landed(buf, kind, j, n):
        other = (1 - c) * 4
        block = (
            lambda: piece(buf, kind, j, from_left),
            lambda: piece(buf, kind, j, from_right),
            lambda: piece(buf, kind, j, far, 0, 32),
            lambda: piece(buf, kind, j, far, 32, 32),
            lambda: piece(buf, kind, j, other + y),
            lambda: piece(buf, kind, j, other + lax.rem(y + 3, 4)),
            lambda: piece(buf, kind, j, other + lax.rem(y + 1, 4)),
            lambda: piece(buf, kind, j, other + lax.rem(y + 2, 4)),
        )[n]()
        remote(block, block, ag_s.at[kind, j, n], ag_r.at[kind, j, n], partner).wait_recv()

    def gather_near(buf, kind, j):
        landed(buf, kind, j, 0)
        gather_copy(buf, kind, j, 2).start()
        gather_copy(buf, kind, j, 5).start()
        landed(buf, kind, j, 1)
        gather_copy(buf, kind, j, 3).start()
        gather_copy(buf, kind, j, 6).start()

    def gather_far(buf, kind, j):
        landed(buf, kind, j, 2)
        landed(buf, kind, j, 3)
        gather_copy(buf, kind, j, 7).start()

    def gather_rest(buf, kind, j):
        for n in (4, 5, 6, 7):
            landed(buf, kind, j, n)

    e_row = routing_ref[...]
    expert_t = iota((16, 128), 0) == e_row
    onehot_t = expert_t.astype(F32)
    before = (iota((128, 128), 0) < iota((128, 128), 1)).astype(BF16)
    earlier = mm(onehot_t.astype(BF16), before)
    slot = jnp.sum(earlier * onehot_t, axis=0, keepdims=True)
    high = (slot >= 4.0).astype(F32) + (slot >= 8.0).astype(F32)
    e_float = e_row.astype(F32)
    target = high * 252.0 + e_float * 16.0 + slot
    tgt_row[y] = target.astype(jnp.int32)
    eye128 = eye_mask(128)

    def to_column(row):
        return jnp.sum(jnp.where(eye128, row, 0.0), axis=1, keepdims=True)

    def to_row(column):
        return jnp.sum(jnp.where(eye128, column, 0.0), axis=0, keepdims=True)

    cols[0] = jnp.broadcast_to(to_column(target), (128, 128))
    cols[1] = jnp.broadcast_to(to_column(e_float), (128, 128))

    def fold_tokens(src, dst, j):
        total = None
        for g in range(GROUPS):
            place = (iota((256, 128), 0) == tgt_row[y] + (4 * g - 256 * j)).astype(BF16)
            term = mm(place, src[:, g * dgw : (g + 1) * dgw])
            total = term if total is None else total + term
        dst[j] = total.astype(BF16).reshape(16, 16, dgw)

    crossing = (
        (crossed.at[y], right),
        (crossed.at[y], left),
        (crossed.at[lax.rem(y + 3, 4), pl.ds(0, 64)], right),
        (crossed.at[lax.rem(y + 1, 4), pl.ds(64, 64)], left),
    )

    def cross_copy(n):
        block, to = crossing[n]
        return remote(block, block, cr_s.at[n], cr_r.at[n], to)

    def target_copy(k):
        to = (d, lax.rem(y + k, 4) * 2 + c)
        return remote(tgt_row.at[y], tgt_row.at[y], cr_s.at[4 + k], cr_r.at[4 + k], to)

    def cross_landed(n):
        block = (
            crossed.at[lax.rem(y + 3, 4)],
            crossed.at[lax.rem(y + 1, 4)],
            crossed.at[lax.rem(y + 2, 4), pl.ds(0, 64)],
            crossed.at[lax.rem(y + 2, 4), pl.ds(64, 64)],
        )[n]
        remote(block, block, cr_s.at[n], cr_r.at[n], right).wait_recv()

    def cross_own():
        for k in (1, 2, 3):
            target_copy(k).start()
        cross_copy(0).start()
        cross_copy(1).start()

    def cross_near():
        cross_landed(0)
        cross_copy(2).start()
        cross_landed(1)
        cross_copy(3).start()

    def cross_far():
        for k in (1, 2, 3):
            block = tgt_row.at[lax.rem(y + 4 - k, 4)]
            remote(block, block, cr_s.at[4 + k], cr_r.at[4 + k], right).wait_recv()
        cross_landed(2)
        cross_landed(3)

    def cross_send(j):
        for g in range(CROSSED):
            total = None
            for p in range(4):
                place = (iota((256, 128), 0) == tgt_row[p] + (4 * p - 256 * j)).astype(BF16)
                term = mm(place, crossed[p, :, g * dgw : (g + 1) * dgw])
                total = term if total is None else total + term
            send_a[g, j] = total.astype(BF16).reshape(16, 16, dgw)
            a2a_start(send_a.at[g], recv_a.at[g], 3 + g, j)

    def cross_pair(j, parity):
        block = full_i.at[j, pl.ds(parity * 4, 4), :, pl.ds(0, cut)]
        return remote(block, block, ca_s.at[j], ca_r.at[j], partner)

    def cross_take(j):
        for g in range(CROSSED):
            a2a_wait(recv_a.at[g], 3 + g, j)
            moved = mm(unfold_m[...], recv_a[g, j].reshape(256, dgw)).astype(BF16)
            full_i[j, pl.ds(c * 4, 4), :, g * dgw : (g + 1) * dgw] = moved.reshape(4, 64, dgw)
        cross_pair(j, c).start()

    out_at = iota((256, 256), 0)
    in_at = iota((256, 256), 1)
    unfold_m[...] = (
        in_at == ((out_at >> 2) & 15) * 16 + (out_at >> 6) * 4 + (out_at & 3)
    ).astype(BF16)
    fold_m[...] = (
        in_at == ((out_at >> 2) & 3) * 64 + (out_at >> 4) * 4 + (out_at & 3)
    ).astype(BF16)

    save_out = iota((384, 384), 0)
    save_m[...] = (
        iota((384, 384), 1)
        == ((save_out >> 2) & 3) * 96
        + (((save_out >> 4) & 3) * 2 + ((save_out >> 6) & 1)) * 12
        + (save_out >> 7) * 4
        + (save_out & 3)
    ).astype(BF16)
    def permute_saved(start, dst):
        @pl.loop(0, 4)
        def _(q):
            block = gab[pl.ds(pl.multiple_of(q * 384, 384), 384), start : start + hidden]
            moved = mm(save_m[...], block).astype(BF16)
            for j in range(CHUNKS):
                for p in range(8):
                    first = (j * 8 + p) * 16
                    dst[j, pl.ds(pl.multiple_of(p * 64 + q * 16, 16), 16), :] = moved[
                        first : first + 16, :
                    ]

    def unfold(src, buf, j):
        moved = mm(unfold_m[...], src[j].reshape(256, dgw)).astype(BF16)
        for g in range(GROUPS):
            buf[j, mine, :, g * dgw : (g + 1) * dgw] = moved[g * 64 : (g + 1) * 64, :]

    def make_hidden(j):
        @pl.loop(0, hidden // 256)
        def _(n):
            at = pl.ds(pl.multiple_of(n * 256, 256), 256)
            a = a_perm[j, :, at].astype(F32)
            b = b_perm[j, :, at].astype(F32)
            value = (a * jax.nn.sigmoid(a) * b).astype(BF16)
            hid_t[at, j * rows : (j + 1) * rows] = value.T

    def compute(j):
        @pl.loop(0, hidden // 256)
        def _(n):
            at = pl.ds(pl.multiple_of(n * 256, 256), 256)
            too = pl.ds(pl.multiple_of(n * 256 + hidden, 256), 256)
            gh = mm(full_g[j].reshape(rows, width), down[at, :], NT)
            a = a_perm[j, :, at].astype(F32)
            b = b_perm[j, :, at].astype(F32)
            sg = jax.nn.sigmoid(a)
            silu = a * sg
            here = pl.ds(j * rows, rows)
            gab[here, at] = (gh * b * sg * (1.0 + a * (1.0 - sg))).astype(BF16)
            gab[here, too] = (gh * silu).astype(BF16)

    def partial(j, parity, n):
        at = pl.ds(pl.multiple_of(j * rows + parity * 256, 256), 256)
        hold = pl.ds(pl.multiple_of(n * dgw, 128), dgw)
        return mm(gab[at, :], weights[hold, :], NT).astype(BF16).reshape(4, 64, dgw)

    def pair_copy(j):
        return remote(send_c, recv_c.at[j], pc_s.at[j], pc_r.at[j], partner)

    def partials(j):
        if j > 0:
            pair_copy(j - 1).wait_send()

        @pl.loop(0, GROUPS)
        def _(n):
            send_c[:, :, pl.ds(pl.multiple_of(n * dgw, 128), dgw)] = partial(j, 1 - c, n)

        pair_copy(j).start()

        @pl.loop(0, GROUPS)
        def _(n):
            own_p[j, :, :, pl.ds(pl.multiple_of(n * dgw, 128), dgw)] = partial(j, c, n)

    y_left = lax.rem(y + 3, 4)
    y_right = lax.rem(y + 1, 4)
    y_far = lax.rem(y + 2, 4)

    def pair_sum(j, at):
        return own_p[j, at].astype(F32) + recv_c[j, at].astype(F32)

    def rs_copy(j, n):
        src, dst, to = (
            (st1_s.at[0], st1_r.at[j, 0], right),
            (st1_s.at[1], st1_r.at[j, 1], left),
            (st2_s.at[0], st2_r.at[j, 0], right),
            (st2_s.at[1], st2_r.at[j, 1], left),
        )[n]
        return remote(src, dst, rs_s.at[j, n], rs_r.at[j, n], to)

    def reduce_far(j):
        pair_copy(j).wait_recv()
        if j > 0:
            rs_copy(j - 1, 0).wait_send()
            rs_copy(j - 1, 1).wait_send()
        total = pair_sum(j, y_far)
        st1_s[0] = total[:32].astype(BF16)
        st1_s[1] = total[32:].astype(BF16)
        rs_copy(j, 0).start()
        rs_copy(j, 1).start()

    def reduce_near(j):
        if j > 0:
            rs_copy(j - 1, 2).wait_send()
            rs_copy(j - 1, 3).wait_send()
        rs_copy(j, 0).wait_recv()
        total = pair_sum(j, y_right)
        st2_s[0, :32] = (total[:32] + st1_r[j, 0].astype(F32)).astype(BF16)
        st2_s[0, 32:] = total[32:].astype(BF16)
        rs_copy(j, 2).start()
        rs_copy(j, 1).wait_recv()
        total = pair_sum(j, y_left)
        st2_s[1, :32] = total[:32].astype(BF16)
        st2_s[1, 32:] = (total[32:] + st1_r[j, 1].astype(F32)).astype(BF16)
        rs_copy(j, 3).start()

    def reduce_last(j):
        rs_copy(j, 2).wait_recv()
        rs_copy(j, 3).wait_recv()
        total = pair_sum(j, y) + st2_r[j, 0].astype(F32) + st2_r[j, 1].astype(F32)
        total = total.astype(BF16)
        token = tok_rows[j].astype(F32)
        score = row_score[j][:, :1]
        grad_score = jnp.sum(token * total.astype(F32), axis=1, keepdims=True)
        grad_logit = grad_score * score * (1.0 - score)
        share = jnp.sum(token * grad_logit, axis=0, keepdims=True)
        if j == 0:
            rx_s[...] = share
        else:
            rx_s[...] += share
        stacked = jnp.concatenate(
            [total[:, g * dgw : (g + 1) * dgw] for g in range(GROUPS)], axis=0
        )
        a2a_drain(send_g, 0, j)
        send_g[j] = mm(fold_m[...], stacked).astype(BF16).reshape(16, 16, dgw)
        a2a_start(send_g, recv_r, 2, j)

    def own_grads(j):
        a2a_wait(recv_g, 0, j)
        moved = mm(unfold_m[...], recv_g[j].reshape(256, dgw)).astype(BF16)
        for g in range(GROUPS):
            full_g[j, mine, :, g * dgw : (g + 1) * dgw] = moved[g * 64 : (g + 1) * 64, :]
        gather_own(full_g, 0, j)

    def own_inputs(j):
        a2a_wait(recv_i, 1, j)
        moved = mm(unfold_m[...], recv_i[j].reshape(256, dgw)).astype(BF16)
        for g in range(GROUPS):
            tok_rows[j, :, g * dgw : (g + 1) * dgw] = moved[g * 64 : (g + 1) * 64, :]
        logits = mm(tok_rows[j], rw[...], NT)
        logit = jnp.sum(jnp.where(iota((64, 16), 1) == d, logits, 0.0), axis=1, keepdims=True)
        score = jax.nn.sigmoid(logit)
        row_score[j] = jnp.broadcast_to(score, (64, 128))
        full_i[j, mine, :, cut:] = (score * tok_rows[j, :, cut:].astype(F32)).astype(BF16)

    loads[0].wait()
    for j in range(CHUNKS):
        fold_tokens(ogr, send_g, j)
        if j == 0:
            pl.semaphore_wait(barrier, 22)
        a2a_start(send_g, recv_g, 0, j)
    for load in loads[3:]:
        load.start()
    loads[1].wait()
    loads[2].wait()
    logits = mm(tok[...], rw[...], NT)
    lane_e = iota((128, 16), 1).astype(F32)
    onehot = (lane_e == cols[1][:, :16]).astype(F32)
    score = jax.nn.sigmoid(jnp.sum(logits * onehot, axis=1, keepdims=True))
    cols[2] = jnp.broadcast_to(score, (128, 128))
    crossed[y] = (score * tok[:, :cut].astype(F32)).astype(BF16)
    cross_own()
    own_grads(0)
    own_grads(1)
    fold_tokens(tok, send_i, 0)
    a2a_start(send_i, recv_i, 1, 0)
    cross_near()
    own_grads(2)
    gather_near(full_g, 0, 0)
    for j in (1, 2):
        fold_tokens(tok, send_i, j)
        a2a_start(send_i, recv_i, 1, j)
    loads[3].wait()
    loads[4].wait()
    permute_saved(0, a_perm)
    gather_near(full_g, 0, 1)
    permute_saved(hidden, b_perm)
    cross_far()
    cross_send(0)
    gather_far(full_g, 0, 0)
    for load in loads[5:]:
        load.wait()
    own_inputs(0)
    gather_near(full_g, 0, 2)
    gather_own(full_i, 1, 0)
    cross_send(1)
    gather_rest(full_g, 0, 0)
    compute(0)
    gather_far(full_g, 0, 1)
    partials(0)
    gather_far(full_g, 0, 2)
    reduce_far(0)
    cross_send(2)
    gather_rest(full_g, 0, 1)
    compute(1)
    partials(1)
    reduce_near(0)
    reduce_far(1)
    gather_rest(full_g, 0, 2)
    compute(2)
    gather_near(full_i, 1, 0)
    partials(2)
    reduce_near(1)
    reduce_far(2)
    own_inputs(1)
    gather_own(full_i, 1, 1)
    reduce_last(0)
    cross_take(0)
    own_inputs(2)
    late_grad = pltpu.make_async_copy(
        gab.at[pl.ds(2 * rows, rows)], late_grad_hbm, out_sem.at[4]
    )
    late_grad.start()
    make_hidden(0)
    make_hidden(1)
    make_hidden(2)
    reduce_near(2)
    gather_far(full_i, 1, 0)
    cross_take(1)
    cross_take(2)

    tile = 512

    @pl.loop(0, width // tile)
    def _(n):
        at = pl.ds(pl.multiple_of(n * tile, tile), tile)
        down[:, at] = mm(hid_t[...], full_g[:, :, :, at].reshape(CHUNKS * rows, tile)).astype(BF16)

    down_out = pltpu.make_async_copy(down, grad_down_hbm, out_sem.at[0])
    down_out.start()
    reduce_last(1)
    gather_near(full_i, 1, 1)
    gather_own(full_i, 1, 2)
    reduce_last(2)

    @pl.loop(1, 8)
    def _(k):
        to = lax.rem(t + k, 8)
        remote(rx_s, rx_r.at[t], rt_s.at[0], rt_r.at[0], (d, to)).start()

    rx_r[t] = rx_s[...]

    def bring_back(j):
        a2a_wait(recv_r, 2, j)
        for g in range(GROUPS):
            part = slice(g * dgw, (g + 1) * dgw)
            wanted = cols[0].astype(jnp.int32)
            wanted = jnp.concatenate([wanted, wanted], axis=1) + (4 * g - 256 * j)
            take = (iota((128, 256), 1) == wanted).astype(BF16)
            moved = mm(take, recv_r[j].reshape(256, dgw))
            if j == 0:
                gs[:, part] = moved
            else:
                gs[:, part] += moved

    bring_back(0)
    bring_back(1)
    bring_back(2)
    gather_far(full_i, 1, 1)
    gather_near(full_i, 1, 2)
    score = cols[2][:, :1]
    grad_score = jnp.zeros((128, 1), F32)
    for g in range(GROUPS):
        part = slice(g * dgw, (g + 1) * dgw)
        grad_score += jnp.sum(tok[:, part].astype(F32) * gs[:, part], axis=1, keepdims=True)
    grad_logit = grad_score * score * (1.0 - score)
    lane_e = iota((128, 16), 1).astype(F32)
    onehot = (lane_e == cols[1][:, :16]).astype(BF16)
    for g in range(GROUPS):
        part = slice(g * dgw, (g + 1) * dgw)
        picked = mm(onehot, rw[:, part])
        ogr[:, part] = (score * gs[:, part] + grad_logit * picked).astype(BF16)
    tokens_out = pltpu.make_async_copy(ogr, grad_tokens_hbm, out_sem.at[1])
    tokens_out.start()

    block = rx_r.at[pl.ds(0, 7)]
    pltpu.make_async_copy(block, block, rt_r.at[0]).wait()
    ry_s[...] = jnp.sum(rx_r[...], axis=0)

    @pl.loop(1, 16)
    def _(k):
        to = lax.rem(d + k, 16)
        remote(ry_s, ry_r.at[d], rt_s.at[1], rt_r.at[1], (to, t)).start()

    ry_r[d] = ry_s[...]

    def early(first, last):
        @pl.loop(first, last)
        def _(n):
            at = pl.ds(pl.multiple_of(n * 256, 256), 256)
            value = mm(full_i[:2, :, :, at].reshape(2 * rows, 256), gab[: 2 * rows, :], TN)
            weights[at, :] = value.astype(BF16)
            pltpu.make_async_copy(
                weights.at[at, :], early_hbm.at[at, :], out_sem.at[2]
            ).start()

    def late_in(p):
        pltpu.make_async_copy(full_i.at[2, p], late_in_hbm.at[p], out_sem.at[3]).start()

    steps = width // 256
    for j in (0, 1):
        gather_rest(full_i, 1, j)
        cross_pair(j, 1 - c).wait_recv()
    early(0, steps // 2)
    gather_far(full_i, 1, 2)
    early(steps // 2, steps)
    cross_pair(2, 1 - c).wait_recv()
    for n in (4, 5, 6):
        landed(full_i, 1, 2, n)
    other = (1 - c) * 4
    late_in(other + y)
    late_in(other + lax.rem(y + 1, 4))
    late_in(other + lax.rem(y + 3, 4))
    for p in range(4):
        late_in(c * 4 + p)
    block = ry_r.at[pl.ds(0, 15)]
    pltpu.make_async_copy(block, block, rt_r.at[1]).wait()
    for k in range(16):
        grad_router_ref[k : k + 1, :] = ry_r[k]
    landed(full_i, 1, 2, 7)
    late_in(other + lax.rem(y + 2, 4))

    down_out.wait()
    tokens_out.wait()
    late_grad.wait()
    pltpu.make_async_copy(weights, early_hbm, out_sem.at[2]).wait()
    pltpu.make_async_copy(full_i.at[2], late_in_hbm, out_sem.at[3]).wait()
    for j in range(CHUNKS):
        a2a_drain(send_i, 1, j)
        a2a_drain(send_g, 2, j)
        for n in range(8):
            gather_copy(full_g, 0, j, n).wait_send()
            gather_copy(full_i, 1, j, n).wait_send()
    for n in range(4):
        cross_copy(n).wait_send()
    for k in (1, 2, 3):
        target_copy(k).wait_send()
    for j in range(CHUNKS):
        cross_pair(j, c).wait_send()
        for g in range(CROSSED):
            a2a_drain(send_a.at[g], 3 + g, j)
    pair_copy(CHUNKS - 1).wait_send()
    for n in range(4):
        rs_copy(CHUNKS - 1, n).wait_send()
    block = rx_r.at[pl.ds(0, 7)]
    pltpu.make_async_copy(block, block, rt_s.at[0]).wait()
    block = ry_r.at[pl.ds(0, 15)]
    pltpu.make_async_copy(block, block, rt_s.at[1]).wait()


def finish(
    early_hbm,
    late_in_hbm,
    late_grad_hbm,
    tokens_in,
    down_in,
    router_in,
    gate_hbm,
    up_hbm,
    tokens_hbm,
    down_hbm,
    router_hbm,
    early,
    late_in,
    late_grad,
    tokens,
    down,
    router,
    gate,
    up,
    in_sem,
    out_sem,
):
    width, hidden = gate.shape
    parts = 5
    step = width // parts
    stripes = [pl.ds(n * step, step) for n in range(parts)]
    moves = [(late_grad_hbm, late_grad), (late_in_hbm, late_in)]
    moves += [(early_hbm.at[at], early.at[at]) for at in stripes]
    moves += [(down_in, down), (tokens_in, tokens), (router_in, router)]
    loads = [pltpu.make_async_copy(a, b, in_sem.at[n]) for n, (a, b) in enumerate(moves)]
    for load in loads:
        load.start()
    stores = []

    def store(src, dst):
        stores.append(pltpu.make_async_copy(src, dst, out_sem.at[len(stores)]))
        stores[-1].start()

    loads[0].wait()
    loads[1].wait()
    for n, at in enumerate(stripes):
        loads[2 + n].wait()
        value = mm(late_in[:, n * step : (n + 1) * step], late_grad[...], TN)
        value = value + early[at, :].astype(F32)
        gate[at, :] = value[:, :hidden].astype(BF16)
        up[at, :] = value[:, hidden:].astype(BF16)
        store(gate.at[at], gate_hbm.at[at])
        store(up.at[at], up_hbm.at[at])
    for n, (src, dst) in enumerate(
        ((down, down_hbm), (tokens, tokens_hbm), (router, router_hbm))
    ):
        loads[2 + parts + n].wait()
        store(src, dst)
    for one in stores:
        one.wait()


def local(
    tokens,
    out_grad,
    routing,
    router_weight,
    gate_weight,
    up_weight,
    down_weight,
    saved_gate,
    saved_up,
):
    count, width = tokens.shape
    experts = router_weight.shape[1]
    slots = saved_gate.shape[1]
    hidden = saved_gate.shape[2]
    per = slots // CHUNKS
    dgw = width // GROUPS
    anywhere = pl.BlockSpec(memory_space=pl.ANY)
    vmem = pl.BlockSpec(memory_space=pltpu.VMEM)
    dma = pltpu.SemaphoreType.DMA
    folded = pltpu.VMEM((CHUNKS, experts, 16, dgw), BF16)
    outs = pl.pallas_call(
        kernel,
        out_shape=(
            jax.ShapeDtypeStruct((count, width), BF16),
            jax.ShapeDtypeStruct((width, 2 * hidden), BF16),
            jax.ShapeDtypeStruct((8, 64, width), BF16),
            jax.ShapeDtypeStruct((per, 2 * hidden), BF16),
            jax.ShapeDtypeStruct((hidden, width), BF16),
            jax.ShapeDtypeStruct((experts, width), F32),
        ),
        in_specs=[vmem] + [anywhere] * 8,
        out_specs=(anywhere, anywhere, anywhere, anywhere, anywhere, vmem),
        scratch_shapes=[
            pltpu.VMEM((count, width), BF16),
            pltpu.VMEM((count, width), BF16),
            pltpu.VMEM((CHUNKS, 64, width), BF16),
            pltpu.VMEM((CHUNKS, 64, 128), F32),
            pltpu.VMEM((experts, width), BF16),
            pltpu.VMEM((width, 2 * hidden), BF16),
            pltpu.VMEM((hidden, width), BF16),
            pltpu.VMEM((CHUNKS, per, hidden), BF16),
            pltpu.VMEM((CHUNKS, per, hidden), BF16),
            pltpu.VMEM((hidden, slots), BF16),
            pltpu.VMEM((slots, 2 * hidden), BF16),
            folded,
            folded,
            folded,
            folded,
            folded,
            pltpu.VMEM((CHUNKS, 8, 64, width), BF16),
            pltpu.VMEM((CHUNKS, 8, 64, width), BF16),
            pltpu.VMEM((4, 64, width), BF16),
            pltpu.VMEM((CHUNKS, 4, 64, width), BF16),
            pltpu.VMEM((CHUNKS, 4, 64, width), BF16),
            pltpu.VMEM((2, 32, width), BF16),
            pltpu.VMEM((CHUNKS, 2, 32, width), BF16),
            pltpu.VMEM((2, 64, width), BF16),
            pltpu.VMEM((CHUNKS, 2, 64, width), BF16),
            pltpu.VMEM((256, 256), BF16),
            pltpu.VMEM((256, 256), BF16),
            pltpu.VMEM((384, 384), BF16),
            pltpu.VMEM((count, width), F32),
            pltpu.VMEM((4, count, CROSSED * dgw), BF16),
            pltpu.VMEM((CROSSED, CHUNKS, experts, 16, dgw), BF16),
            pltpu.VMEM((CROSSED, CHUNKS, experts, 16, dgw), BF16),
            pltpu.VMEM((4, 1, 128), jnp.int32),
            pltpu.VMEM((3, 128, 128), F32),
            pltpu.VMEM((1, width), F32),
            pltpu.VMEM((8, 1, width), F32),
            pltpu.VMEM((1, width), F32),
            pltpu.VMEM((16, 1, width), F32),
            dma((8,)),
            dma((3 + CROSSED, CHUNKS)),
            dma((3 + CROSSED, CHUNKS)),
            dma((8,)),
            dma((8,)),
            dma((CHUNKS,)),
            dma((CHUNKS,)),
            dma((2, CHUNKS, 8)),
            dma((2, CHUNKS, 8)),
            dma((CHUNKS,)),
            dma((CHUNKS,)),
            dma((CHUNKS, 4)),
            dma((CHUNKS, 4)),
            dma((2,)),
            dma((2,)),
            dma((5,)),
        ],
        compiler_params=pltpu.CompilerParams(
            collective_id=0, has_side_effects=True, vmem_limit_bytes=63 * 2**20
        ),
        cost_estimate=pl.CostEstimate(
            flops=12 * slots * width * hidden,
            bytes_accessed=2 * (6 * width * hidden + 2 * slots * hidden + 4 * count * width),
            transcendentals=slots * hidden,
        ),
    )(
        routing.reshape(1, count),
        tokens,
        out_grad,
        router_weight.T,
        gate_weight[0],
        up_weight[0],
        down_weight[0],
        saved_gate[0],
        saved_up[0],
    )
    grad_tokens, early, late_in, late_grad, grad_down, grad_router = outs
    grad_gate, grad_up, grad_tokens, grad_down, grad_router = pl.pallas_call(
        finish,
        out_shape=(
            jax.ShapeDtypeStruct((width, hidden), BF16),
            jax.ShapeDtypeStruct((width, hidden), BF16),
            jax.ShapeDtypeStruct((count, width), BF16),
            jax.ShapeDtypeStruct((hidden, width), BF16),
            jax.ShapeDtypeStruct((experts, width), F32),
        ),
        in_specs=[anywhere] * 6,
        out_specs=(anywhere,) * 5,
        scratch_shapes=[
            pltpu.VMEM((width, 2 * hidden), BF16),
            pltpu.VMEM((per, width), BF16),
            pltpu.VMEM((per, 2 * hidden), BF16),
            pltpu.VMEM((count, width), BF16),
            pltpu.VMEM((hidden, width), BF16),
            pltpu.VMEM((experts, width), F32),
            pltpu.VMEM((width, hidden), BF16),
            pltpu.VMEM((width, hidden), BF16),
            dma((10,)),
            dma((13,)),
        ],
        compiler_params=pltpu.CompilerParams(vmem_limit_bytes=62 * 2**20),
    )(early, late_in.reshape(per, width), late_grad, grad_tokens, grad_down, grad_router)
    return grad_tokens, grad_gate[None], grad_up[None], grad_down[None], grad_router.T


def solution(mesh):
    placed = (
        P(("dp", "tensor"), None),
        P(("dp", "tensor"), None),
        P(("dp", "tensor"), None),
        P(),
        P("dp", None, "tensor"),
        P("dp", None, "tensor"),
        P("dp", "tensor", None),
        P("dp", None, "tensor"),
        P("dp", None, "tensor"),
    )
    return jax.shard_map(
        local,
        mesh=mesh,
        in_specs=placed,
        out_specs=(
            P(("dp", "tensor"), None),
            P("dp", None, "tensor"),
            P("dp", None, "tensor"),
            P("dp", "tensor", None),
            P(),
        ),
        check_vma=False,
    )
```

```python
import jax
import jax.numpy as jnp
from jax import lax
from jax.experimental import pallas as pl
from jax.experimental.pallas import tpu as pltpu
from jax.sharding import PartitionSpec as P

MESH = pl.DeviceIdType.MESH
NN = (((1,), (0,)), ((), ()))
NT = (((1,), (1,)), ((), ()))
TN = (((0,), (0,)), ((), ()))
F32 = jnp.float32
BF16 = jnp.bfloat16

CHUNKS = 3
GROUPS = 4
CROSSED = 1


def mm(a, b, dims=NN):
    return lax.dot_general(a, b, dims, preferred_element_type=F32)


def iota(shape, dim):
    return lax.broadcasted_iota(jnp.int32, shape, dim)


def eye_mask(n):
    return iota((n, n), 0) == iota((n, n), 1)


def kernel(
    routing_ref,
    tokens_hbm,
    out_grad_hbm,
    router_hbm,
    gate_hbm,
    up_hbm,
    down_hbm,
    saved_gate_hbm,
    saved_up_hbm,
    grad_tokens_hbm,
    early_hbm,
    late_in_hbm,
    late_grad_hbm,
    grad_down_hbm,
    grad_router_ref,
    tok,
    ogr,
    tok_rows,
    row_score,
    rw,
    weights,
    down,
    a_perm,
    b_perm,
    hid_t,
    gab,
    send_g,
    send_i,
    recv_g,
    recv_i,
    recv_r,
    full_g,
    full_i,
    send_c,
    own_p,
    recv_c,
    st1_s,
    st1_r,
    st2_s,
    st2_r,
    unfold_m,
    fold_m,
    save_m,
    gs,
    crossed,
    send_a,
    recv_a,
    tgt_row,
    cols,
    rx_s,
    rx_r,
    ry_s,
    ry_r,
    load_sem,
    a2a_s,
    a2a_r,
    cr_s,
    cr_r,
    ca_s,
    ca_r,
    ag_s,
    ag_r,
    pc_s,
    pc_r,
    rs_s,
    rs_r,
    rt_s,
    rt_r,
    out_sem,
):
    d = lax.axis_index("dp")
    t = lax.axis_index("tensor")
    y = t // 2
    c = lax.rem(t, 2)
    right = (d, lax.rem(y + 1, 4) * 2 + c)
    left = (d, lax.rem(y + 3, 4) * 2 + c)
    partner = (d, y * 2 + 1 - c)
    mine = c * 4 + y
    from_left = c * 4 + lax.rem(y + 3, 4)
    from_right = c * 4 + lax.rem(y + 1, 4)
    far = c * 4 + lax.rem(y + 2, 4)
    dgw = tok.shape[1] // GROUPS
    rows = full_g.shape[1] * full_g.shape[2]
    width = tok.shape[1]
    hidden = down.shape[0]
    cut = CROSSED * dgw

    loads = [
        pltpu.make_async_copy(src, dst, load_sem.at[n])
        for n, (src, dst) in enumerate(
            (
                (out_grad_hbm, ogr),
                (tokens_hbm, tok),
                (router_hbm, rw),
                (saved_gate_hbm, gab.at[:, pl.ds(0, hidden)]),
                (saved_up_hbm, gab.at[:, pl.ds(hidden, hidden)]),
                (down_hbm, down),
                (gate_hbm, weights.at[:, pl.ds(0, hidden)]),
                (up_hbm, weights.at[:, pl.ds(hidden, hidden)]),
            )
        )
    ]
    for load in loads[:3]:
        load.start()

    barrier = pltpu.get_barrier_semaphore()

    @pl.loop(1, 16)
    def _(k):
        pl.semaphore_signal(
            barrier, inc=1, device_id=(lax.rem(d + k, 16), t), device_id_type=MESH
        )

    @pl.loop(1, 8)
    def _(k):
        pl.semaphore_signal(
            barrier, inc=1, device_id=(d, lax.rem(t + k, 8)), device_id_type=MESH
        )

    def remote(src, dst, send_sem, recv_sem, to):
        return pltpu.make_async_remote_copy(
            src_ref=src,
            dst_ref=dst,
            send_sem=send_sem,
            recv_sem=recv_sem,
            device_id=to,
            device_id_type=MESH,
        )

    def a2a_start(src, dst, kind, j):
        @pl.loop(1, 16)
        def _(k):
            to = lax.rem(d + k, 16)
            remote(
                src.at[j, to], dst.at[j, d], a2a_s.at[kind, j], a2a_r.at[kind, j], (to, t)
            ).start()

        dst[j, d] = src[j, d]

    def a2a_wait(dst, kind, j):
        part = dst.at[j, pl.ds(0, 15)]
        pltpu.make_async_copy(part, part, a2a_r.at[kind, j]).wait()

    def a2a_drain(src, kind, j):
        part = src.at[j, pl.ds(0, 15)]
        pltpu.make_async_copy(part, part, a2a_s.at[kind, j]).wait()

    def piece(buf, kind, j, p, first=0, count=64):
        if kind == 0:
            return buf.at[j, p, pl.ds(first, count)]
        return buf.at[j, p, pl.ds(first, count), pl.ds(cut, width - cut)]

    def gather_copy(buf, kind, j, n):
        block, to = (
            (piece(buf, kind, j, mine), right),
            (piece(buf, kind, j, mine), left),
            (piece(buf, kind, j, from_left, 0, 32), right),
            (piece(buf, kind, j, from_right, 32, 32), left),
            (piece(buf, kind, j, mine), partner),
            (piece(buf, kind, j, from_left), partner),
            (piece(buf, kind, j, from_right), partner),
            (piece(buf, kind, j, far), partner),
        )[n]
        return remote(block, block, ag_s.at[kind, j, n], ag_r.at[kind, j, n], to)

    def gather_own(buf, kind, j):
        for n in (0, 1, 4):
            gather_copy(buf, kind, j, n).start()

    def landed(buf, kind, j, n):
        other = (1 - c) * 4
        block = (
            lambda: piece(buf, kind, j, from_left),
            lambda: piece(buf, kind, j, from_right),
            lambda: piece(buf, kind, j, far, 0, 32),
            lambda: piece(buf, kind, j, far, 32, 32),
            lambda: piece(buf, kind, j, other + y),
            lambda: piece(buf, kind, j, other + lax.rem(y + 3, 4)),
            lambda: piece(buf, kind, j, other + lax.rem(y + 1, 4)),
            lambda: piece(buf, kind, j, other + lax.rem(y + 2, 4)),
        )[n]()
        remote(block, block, ag_s.at[kind, j, n], ag_r.at[kind, j, n], partner).wait_recv()

    def gather_near(buf, kind, j):
        landed(buf, kind, j, 0)
        gather_copy(buf, kind, j, 2).start()
        gather_copy(buf, kind, j, 5).start()
        landed(buf, kind, j, 1)
        gather_copy(buf, kind, j, 3).start()
        gather_copy(buf, kind, j, 6).start()

    def gather_far(buf, kind, j):
        landed(buf, kind, j, 2)
        landed(buf, kind, j, 3)
        gather_copy(buf, kind, j, 7).start()

    def gather_rest(buf, kind, j):
        for n in (4, 5, 6, 7):
            landed(buf, kind, j, n)

    e_row = routing_ref[...]
    expert_t = iota((16, 128), 0) == e_row
    onehot_t = expert_t.astype(F32)
    before = (iota((128, 128), 0) < iota((128, 128), 1)).astype(BF16)
    earlier = mm(onehot_t.astype(BF16), before)
    slot = jnp.sum(earlier * onehot_t, axis=0, keepdims=True)
    high = (slot >= 4.0).astype(F32) + (slot >= 8.0).astype(F32)
    e_float = e_row.astype(F32)
    target = high * 252.0 + e_float * 16.0 + slot
    tgt_row[y] = target.astype(jnp.int32)
    eye128 = eye_mask(128)

    def to_column(row):
        return jnp.sum(jnp.where(eye128, row, 0.0), axis=1, keepdims=True)

    def to_row(column):
        return jnp.sum(jnp.where(eye128, column, 0.0), axis=0, keepdims=True)

    cols[0] = jnp.broadcast_to(to_column(target), (128, 128))
    cols[1] = jnp.broadcast_to(to_column(e_float), (128, 128))

    def fold_tokens(src, dst, j):
        total = None
        for g in range(GROUPS):
            place = (iota((256, 128), 0) == tgt_row[y] + (4 * g - 256 * j)).astype(BF16)
            term = mm(place, src[:, g * dgw : (g + 1) * dgw])
            total = term if total is None else total + term
        dst[j] = total.astype(BF16).reshape(16, 16, dgw)

    crossing = (
        (crossed.at[y], right),
        (crossed.at[y], left),
        (crossed.at[lax.rem(y + 3, 4), pl.ds(0, 64)], right),
        (crossed.at[lax.rem(y + 1, 4), pl.ds(64, 64)], left),
    )

    def cross_copy(n):
        block, to = crossing[n]
        return remote(block, block, cr_s.at[n], cr_r.at[n], to)

    def target_copy(k):
        to = (d, lax.rem(y + k, 4) * 2 + c)
        return remote(tgt_row.at[y], tgt_row.at[y], cr_s.at[4 + k], cr_r.at[4 + k], to)

    def cross_landed(n):
        block = (
            crossed.at[lax.rem(y + 3, 4)],
            crossed.at[lax.rem(y + 1, 4)],
            crossed.at[lax.rem(y + 2, 4), pl.ds(0, 64)],
            crossed.at[lax.rem(y + 2, 4), pl.ds(64, 64)],
        )[n]
        remote(block, block, cr_s.at[n], cr_r.at[n], right).wait_recv()

    def cross_own():
        for k in (1, 2, 3):
            target_copy(k).start()
        cross_copy(0).start()
        cross_copy(1).start()

    def cross_near():
        cross_landed(0)
        cross_copy(2).start()
        cross_landed(1)
        cross_copy(3).start()

    def cross_far():
        for k in (1, 2, 3):
            block = tgt_row.at[lax.rem(y + 4 - k, 4)]
            remote(block, block, cr_s.at[4 + k], cr_r.at[4 + k], right).wait_recv()
        cross_landed(2)
        cross_landed(3)

    def cross_send(j):
        for g in range(CROSSED):
            total = None
            for p in range(4):
                place = (iota((256, 128), 0) == tgt_row[p] + (4 * p - 256 * j)).astype(BF16)
                term = mm(place, crossed[p, :, g * dgw : (g + 1) * dgw])
                total = term if total is None else total + term
            send_a[g, j] = total.astype(BF16).reshape(16, 16, dgw)
            a2a_start(send_a.at[g], recv_a.at[g], 3 + g, j)

    def cross_pair(j, parity):
        block = full_i.at[j, pl.ds(parity * 4, 4), :, pl.ds(0, cut)]
        return remote(block, block, ca_s.at[j], ca_r.at[j], partner)

    def cross_take(j):
        for g in range(CROSSED):
            a2a_wait(recv_a.at[g], 3 + g, j)
            moved = mm(unfold_m[...], recv_a[g, j].reshape(256, dgw)).astype(BF16)
            full_i[j, pl.ds(c * 4, 4), :, g * dgw : (g + 1) * dgw] = moved.reshape(4, 64, dgw)
        cross_pair(j, c).start()

    out_at = iota((256, 256), 0)
    in_at = iota((256, 256), 1)
    unfold_m[...] = (
        in_at == ((out_at >> 2) & 15) * 16 + (out_at >> 6) * 4 + (out_at & 3)
    ).astype(BF16)
    fold_m[...] = (
        in_at == ((out_at >> 2) & 3) * 64 + (out_at >> 4) * 4 + (out_at & 3)
    ).astype(BF16)

    save_out = iota((384, 384), 0)
    save_m[...] = (
        iota((384, 384), 1)
        == ((save_out >> 2) & 3) * 96
        + (((save_out >> 4) & 3) * 2 + ((save_out >> 6) & 1)) * 12
        + (save_out >> 7) * 4
        + (save_out & 3)
    ).astype(BF16)
    def permute_saved(start, dst):
        @pl.loop(0, 4)
        def _(q):
            block = gab[pl.ds(pl.multiple_of(q * 384, 384), 384), start : start + hidden]
            moved = mm(save_m[...], block).astype(BF16)
            for j in range(CHUNKS):
                for p in range(8):
                    first = (j * 8 + p) * 16
                    dst[j, pl.ds(pl.multiple_of(p * 64 + q * 16, 16), 16), :] = moved[
                        first : first + 16, :
                    ]

    def unfold(src, buf, j):
        moved = mm(unfold_m[...], src[j].reshape(256, dgw)).astype(BF16)
        for g in range(GROUPS):
            buf[j, mine, :, g * dgw : (g + 1) * dgw] = moved[g * 64 : (g + 1) * 64, :]

    def make_hidden(j):
        @pl.loop(0, hidden // 256)
        def _(n):
            at = pl.ds(pl.multiple_of(n * 256, 256), 256)
            a = a_perm[j, :, at].astype(F32)
            b = b_perm[j, :, at].astype(F32)
            value = (a * jax.nn.sigmoid(a) * b).astype(BF16)
            hid_t[at, j * rows : (j + 1) * rows] = value.T

    def compute(j):
        @pl.loop(0, hidden // 256)
        def _(n):
            at = pl.ds(pl.multiple_of(n * 256, 256), 256)
            too = pl.ds(pl.multiple_of(n * 256 + hidden, 256), 256)
            gh = mm(full_g[j].reshape(rows, width), down[at, :], NT)
            a = a_perm[j, :, at].astype(F32)
            b = b_perm[j, :, at].astype(F32)
            sg = jax.nn.sigmoid(a)
            silu = a * sg
            here = pl.ds(j * rows, rows)
            gab[here, at] = (gh * b * sg * (1.0 + a * (1.0 - sg))).astype(BF16)
            gab[here, too] = (gh * silu).astype(BF16)

    def partial(j, parity, n):
        at = pl.ds(pl.multiple_of(j * rows + parity * 256, 256), 256)
        hold = pl.ds(pl.multiple_of(n * dgw, 128), dgw)
        return mm(gab[at, :], weights[hold, :], NT).astype(BF16).reshape(4, 64, dgw)

    def pair_copy(j):
        return remote(send_c, recv_c.at[j], pc_s.at[j], pc_r.at[j], partner)

    def partials(j):
        if j > 0:
            pair_copy(j - 1).wait_send()

        @pl.loop(0, GROUPS)
        def _(n):
            send_c[:, :, pl.ds(pl.multiple_of(n * dgw, 128), dgw)] = partial(j, 1 - c, n)

        pair_copy(j).start()

        @pl.loop(0, GROUPS)
        def _(n):
            own_p[j, :, :, pl.ds(pl.multiple_of(n * dgw, 128), dgw)] = partial(j, c, n)

    y_left = lax.rem(y + 3, 4)
    y_right = lax.rem(y + 1, 4)
    y_far = lax.rem(y + 2, 4)

    def pair_sum(j, at):
        return own_p[j, at].astype(F32) + recv_c[j, at].astype(F32)

    def rs_copy(j, n):
        src, dst, to = (
            (st1_s.at[0], st1_r.at[j, 0], right),
            (st1_s.at[1], st1_r.at[j, 1], left),
            (st2_s.at[0], st2_r.at[j, 0], right),
            (st2_s.at[1], st2_r.at[j, 1], left),
        )[n]
        return remote(src, dst, rs_s.at[j, n], rs_r.at[j, n], to)

    def reduce_far(j):
        pair_copy(j).wait_recv()
        if j > 0:
            rs_copy(j - 1, 0).wait_send()
            rs_copy(j - 1, 1).wait_send()
        total = pair_sum(j, y_far)
        st1_s[0] = total[:32].astype(BF16)
        st1_s[1] = total[32:].astype(BF16)
        rs_copy(j, 0).start()
        rs_copy(j, 1).start()

    def reduce_near(j):
        if j > 0:
            rs_copy(j - 1, 2).wait_send()
            rs_copy(j - 1, 3).wait_send()
        rs_copy(j, 0).wait_recv()
        total = pair_sum(j, y_right)
        st2_s[0, :32] = (total[:32] + st1_r[j, 0].astype(F32)).astype(BF16)
        st2_s[0, 32:] = total[32:].astype(BF16)
        rs_copy(j, 2).start()
        rs_copy(j, 1).wait_recv()
        total = pair_sum(j, y_left)
        st2_s[1, :32] = total[:32].astype(BF16)
        st2_s[1, 32:] = (total[32:] + st1_r[j, 1].astype(F32)).astype(BF16)
        rs_copy(j, 3).start()

    def reduce_last(j):
        rs_copy(j, 2).wait_recv()
        rs_copy(j, 3).wait_recv()
        total = pair_sum(j, y) + st2_r[j, 0].astype(F32) + st2_r[j, 1].astype(F32)
        total = total.astype(BF16)
        token = tok_rows[j].astype(F32)
        score = row_score[j][:, :1]
        grad_score = jnp.sum(token * total.astype(F32), axis=1, keepdims=True)
        grad_logit = grad_score * score * (1.0 - score)
        share = jnp.sum(token * grad_logit, axis=0, keepdims=True)
        if j == 0:
            rx_s[...] = share
        else:
            rx_s[...] += share
        stacked = jnp.concatenate(
            [total[:, g * dgw : (g + 1) * dgw] for g in range(GROUPS)], axis=0
        )
        a2a_drain(send_g, 0, j)
        send_g[j] = mm(fold_m[...], stacked).astype(BF16).reshape(16, 16, dgw)
        a2a_start(send_g, recv_r, 2, j)

    def own_grads(j):
        a2a_wait(recv_g, 0, j)
        moved = mm(unfold_m[...], recv_g[j].reshape(256, dgw)).astype(BF16)
        for g in range(GROUPS):
            full_g[j, mine, :, g * dgw : (g + 1) * dgw] = moved[g * 64 : (g + 1) * 64, :]
        gather_own(full_g, 0, j)

    def own_inputs(j):
        a2a_wait(recv_i, 1, j)
        moved = mm(unfold_m[...], recv_i[j].reshape(256, dgw)).astype(BF16)
        for g in range(GROUPS):
            tok_rows[j, :, g * dgw : (g + 1) * dgw] = moved[g * 64 : (g + 1) * 64, :]
        logits = mm(tok_rows[j], rw[...], NT)
        logit = jnp.sum(jnp.where(iota((64, 16), 1) == d, logits, 0.0), axis=1, keepdims=True)
        score = jax.nn.sigmoid(logit)
        row_score[j] = jnp.broadcast_to(score, (64, 128))
        full_i[j, mine, :, cut:] = (score * tok_rows[j, :, cut:].astype(F32)).astype(BF16)

    loads[0].wait()
    for j in range(CHUNKS):
        fold_tokens(ogr, send_g, j)
        if j == 0:
            pl.semaphore_wait(barrier, 22)
        a2a_start(send_g, recv_g, 0, j)
    for load in loads[3:]:
        load.start()
    loads[1].wait()
    loads[2].wait()
    logits = mm(tok[...], rw[...], NT)
    lane_e = iota((128, 16), 1).astype(F32)
    onehot = (lane_e == cols[1][:, :16]).astype(F32)
    score = jax.nn.sigmoid(jnp.sum(logits * onehot, axis=1, keepdims=True))
    cols[2] = jnp.broadcast_to(score, (128, 128))
    crossed[y] = (score * tok[:, :cut].astype(F32)).astype(BF16)
    cross_own()
    own_grads(0)
    own_grads(1)
    fold_tokens(tok, send_i, 0)
    a2a_start(send_i, recv_i, 1, 0)
    cross_near()
    own_grads(2)
    gather_near(full_g, 0, 0)
    for j in (1, 2):
        fold_tokens(tok, send_i, j)
        a2a_start(send_i, recv_i, 1, j)
    loads[3].wait()
    loads[4].wait()
    permute_saved(0, a_perm)
    gather_near(full_g, 0, 1)
    permute_saved(hidden, b_perm)
    cross_far()
    cross_send(0)
    gather_far(full_g, 0, 0)
    for load in loads[5:]:
        load.wait()
    own_inputs(0)
    gather_near(full_g, 0, 2)
    gather_own(full_i, 1, 0)
    cross_send(1)
    gather_rest(full_g, 0, 0)
    compute(0)
    gather_far(full_g, 0, 1)
    partials(0)
    reduce_far(0)
    gather_far(full_g, 0, 2)
    cross_send(2)
    gather_rest(full_g, 0, 1)
    compute(1)
    reduce_near(0)
    partials(1)
    reduce_far(1)
    gather_rest(full_g, 0, 2)
    compute(2)
    gather_near(full_i, 1, 0)
    reduce_near(1)
    partials(2)
    reduce_far(2)
    own_inputs(1)
    gather_own(full_i, 1, 1)
    reduce_last(0)
    cross_take(0)
    own_inputs(2)
    late_grad = pltpu.make_async_copy(
        gab.at[pl.ds(2 * rows, rows)], late_grad_hbm, out_sem.at[4]
    )
    late_grad.start()
    make_hidden(0)
    make_hidden(1)
    make_hidden(2)
    reduce_near(2)
    gather_far(full_i, 1, 0)
    cross_take(1)
    cross_take(2)
    tile = 512

    @pl.loop(0, width // tile)
    def _(n):
        at = pl.ds(pl.multiple_of(n * tile, tile), tile)
        down[:, at] = mm(hid_t[...], full_g[:, :, :, at].reshape(CHUNKS * rows, tile)).astype(BF16)

    down_out = pltpu.make_async_copy(down, grad_down_hbm, out_sem.at[0])
    down_out.start()
    reduce_last(1)
    gather_near(full_i, 1, 1)
    gather_own(full_i, 1, 2)
    reduce_last(2)
    @pl.loop(1, 8)
    def _(k):
        to = lax.rem(t + k, 8)
        remote(rx_s, rx_r.at[t], rt_s.at[0], rt_r.at[0], (d, to)).start()

    rx_r[t] = rx_s[...]

    def bring_back(j):
        a2a_wait(recv_r, 2, j)
        for g in range(GROUPS):
            part = slice(g * dgw, (g + 1) * dgw)
            wanted = cols[0].astype(jnp.int32)
            wanted = jnp.concatenate([wanted, wanted], axis=1) + (4 * g - 256 * j)
            take = (iota((128, 256), 1) == wanted).astype(BF16)
            moved = mm(take, recv_r[j].reshape(256, dgw))
            if j == 0:
                gs[:, part] = moved
            else:
                gs[:, part] += moved

    def early(first, last):
        @pl.loop(first, last)
        def _(n):
            at = pl.ds(pl.multiple_of(n * 256, 256), 256)
            value = mm(full_i[:2, :, :, at].reshape(2 * rows, 256), gab[: 2 * rows, :], TN)
            weights[at, :] = value.astype(BF16)
            pltpu.make_async_copy(
                weights.at[at, :], early_hbm.at[at, :], out_sem.at[2]
            ).start()

    def late_in(p):
        pltpu.make_async_copy(full_i.at[2, p], late_in_hbm.at[p], out_sem.at[3]).start()

    steps = width // 256
    bring_back(0)
    bring_back(1)
    bring_back(2)
    gather_far(full_i, 1, 1)
    gather_near(full_i, 1, 2)
    score = cols[2][:, :1]
    grad_score = jnp.zeros((128, 1), F32)
    for g in range(GROUPS):
        part = slice(g * dgw, (g + 1) * dgw)
        grad_score += jnp.sum(tok[:, part].astype(F32) * gs[:, part], axis=1, keepdims=True)
    grad_logit = grad_score * score * (1.0 - score)
    lane_e = iota((128, 16), 1).astype(F32)
    onehot = (lane_e == cols[1][:, :16]).astype(BF16)
    for g in range(GROUPS):
        part = slice(g * dgw, (g + 1) * dgw)
        picked = mm(onehot, rw[:, part])
        ogr[:, part] = (score * gs[:, part] + grad_logit * picked).astype(BF16)
    tokens_out = pltpu.make_async_copy(ogr, grad_tokens_hbm, out_sem.at[1])
    tokens_out.start()

    block = rx_r.at[pl.ds(0, 7)]
    pltpu.make_async_copy(block, block, rt_r.at[0]).wait()
    ry_s[...] = jnp.sum(rx_r[...], axis=0)

    @pl.loop(1, 16)
    def _(k):
        to = lax.rem(d + k, 16)
        remote(ry_s, ry_r.at[d], rt_s.at[1], rt_r.at[1], (to, t)).start()

    ry_r[d] = ry_s[...]

    gather_rest(full_i, 1, 0)
    cross_pair(0, 1 - c).wait_recv()
    gather_rest(full_i, 1, 1)
    cross_pair(1, 1 - c).wait_recv()
    early(0, steps // 2)
    gather_far(full_i, 1, 2)
    early(steps // 2, steps)
    cross_pair(2, 1 - c).wait_recv()
    for n in (4, 5, 6):
        landed(full_i, 1, 2, n)
    other = (1 - c) * 4
    late_in(other + y)
    late_in(other + lax.rem(y + 1, 4))
    late_in(other + lax.rem(y + 3, 4))
    for p in range(4):
        late_in(c * 4 + p)
    block = ry_r.at[pl.ds(0, 15)]
    pltpu.make_async_copy(block, block, rt_r.at[1]).wait()
    for k in range(16):
        grad_router_ref[k : k + 1, :] = ry_r[k]
    landed(full_i, 1, 2, 7)
    late_in(other + lax.rem(y + 2, 4))

    down_out.wait()
    tokens_out.wait()
    late_grad.wait()
    pltpu.make_async_copy(weights, early_hbm, out_sem.at[2]).wait()
    pltpu.make_async_copy(full_i.at[2], late_in_hbm, out_sem.at[3]).wait()
    for j in range(CHUNKS):
        a2a_drain(send_i, 1, j)
        a2a_drain(send_g, 2, j)
        for n in range(8):
            gather_copy(full_g, 0, j, n).wait_send()
            gather_copy(full_i, 1, j, n).wait_send()
    for n in range(4):
        cross_copy(n).wait_send()
    for k in (1, 2, 3):
        target_copy(k).wait_send()
    for j in range(CHUNKS):
        cross_pair(j, c).wait_send()
        for g in range(CROSSED):
            a2a_drain(send_a.at[g], 3 + g, j)
    pair_copy(CHUNKS - 1).wait_send()
    for n in range(4):
        rs_copy(CHUNKS - 1, n).wait_send()
    block = rx_r.at[pl.ds(0, 7)]
    pltpu.make_async_copy(block, block, rt_s.at[0]).wait()
    block = ry_r.at[pl.ds(0, 15)]
    pltpu.make_async_copy(block, block, rt_s.at[1]).wait()


def finish(
    early_hbm,
    late_in_hbm,
    late_grad_hbm,
    tokens_in,
    down_in,
    router_in,
    gate_hbm,
    up_hbm,
    tokens_hbm,
    down_hbm,
    router_hbm,
    early,
    late_in,
    late_grad,
    tokens,
    down,
    router,
    gate,
    up,
    in_sem,
    out_sem,
):
    width, hidden = gate.shape
    parts = 5
    step = width // parts
    stripes = [pl.ds(n * step, step) for n in range(parts)]
    moves = [(late_grad_hbm, late_grad), (late_in_hbm, late_in)]
    moves += [(early_hbm.at[at], early.at[at]) for at in stripes]
    moves += [(down_in, down), (tokens_in, tokens), (router_in, router)]
    loads = [pltpu.make_async_copy(a, b, in_sem.at[n]) for n, (a, b) in enumerate(moves)]
    for load in loads:
        load.start()
    stores = []

    def store(src, dst):
        stores.append(pltpu.make_async_copy(src, dst, out_sem.at[len(stores)]))
        stores[-1].start()

    loads[0].wait()
    loads[1].wait()
    for n, at in enumerate(stripes):
        loads[2 + n].wait()
        value = mm(late_in[:, n * step : (n + 1) * step], late_grad[...], TN)
        value = value + early[at, :].astype(F32)
        gate[at, :] = value[:, :hidden].astype(BF16)
        up[at, :] = value[:, hidden:].astype(BF16)
        store(gate.at[at], gate_hbm.at[at])
        store(up.at[at], up_hbm.at[at])
    for n, (src, dst) in enumerate(
        ((down, down_hbm), (tokens, tokens_hbm), (router, router_hbm))
    ):
        loads[2 + parts + n].wait()
        store(src, dst)
    for one in stores:
        one.wait()


def local(
    tokens,
    out_grad,
    routing,
    router_weight,
    gate_weight,
    up_weight,
    down_weight,
    saved_gate,
    saved_up,
):
    count, width = tokens.shape
    experts = router_weight.shape[1]
    slots = saved_gate.shape[1]
    hidden = saved_gate.shape[2]
    per = slots // CHUNKS
    dgw = width // GROUPS
    anywhere = pl.BlockSpec(memory_space=pl.ANY)
    vmem = pl.BlockSpec(memory_space=pltpu.VMEM)
    dma = pltpu.SemaphoreType.DMA
    folded = pltpu.VMEM((CHUNKS, experts, 16, dgw), BF16)
    outs = pl.pallas_call(
        kernel,
        out_shape=(
            jax.ShapeDtypeStruct((count, width), BF16),
            jax.ShapeDtypeStruct((width, 2 * hidden), BF16),
            jax.ShapeDtypeStruct((8, 64, width), BF16),
            jax.ShapeDtypeStruct((per, 2 * hidden), BF16),
            jax.ShapeDtypeStruct((hidden, width), BF16),
            jax.ShapeDtypeStruct((experts, width), F32),
        ),
        in_specs=[vmem] + [anywhere] * 8,
        out_specs=(anywhere, anywhere, anywhere, anywhere, anywhere, vmem),
        scratch_shapes=[
            pltpu.VMEM((count, width), BF16),
            pltpu.VMEM((count, width), BF16),
            pltpu.VMEM((CHUNKS, 64, width), BF16),
            pltpu.VMEM((CHUNKS, 64, 128), F32),
            pltpu.VMEM((experts, width), BF16),
            pltpu.VMEM((width, 2 * hidden), BF16),
            pltpu.VMEM((hidden, width), BF16),
            pltpu.VMEM((CHUNKS, per, hidden), BF16),
            pltpu.VMEM((CHUNKS, per, hidden), BF16),
            pltpu.VMEM((hidden, slots), BF16),
            pltpu.VMEM((slots, 2 * hidden), BF16),
            folded,
            folded,
            folded,
            folded,
            folded,
            pltpu.VMEM((CHUNKS, 8, 64, width), BF16),
            pltpu.VMEM((CHUNKS, 8, 64, width), BF16),
            pltpu.VMEM((4, 64, width), BF16),
            pltpu.VMEM((CHUNKS, 4, 64, width), BF16),
            pltpu.VMEM((CHUNKS, 4, 64, width), BF16),
            pltpu.VMEM((2, 32, width), BF16),
            pltpu.VMEM((CHUNKS, 2, 32, width), BF16),
            pltpu.VMEM((2, 64, width), BF16),
            pltpu.VMEM((CHUNKS, 2, 64, width), BF16),
            pltpu.VMEM((256, 256), BF16),
            pltpu.VMEM((256, 256), BF16),
            pltpu.VMEM((384, 384), BF16),
            pltpu.VMEM((count, width), F32),
            pltpu.VMEM((4, count, CROSSED * dgw), BF16),
            pltpu.VMEM((CROSSED, CHUNKS, experts, 16, dgw), BF16),
            pltpu.VMEM((CROSSED, CHUNKS, experts, 16, dgw), BF16),
            pltpu.VMEM((4, 1, 128), jnp.int32),
            pltpu.VMEM((3, 128, 128), F32),
            pltpu.VMEM((1, width), F32),
            pltpu.VMEM((8, 1, width), F32),
            pltpu.VMEM((1, width), F32),
            pltpu.VMEM((16, 1, width), F32),
            dma((8,)),
            dma((3 + CROSSED, CHUNKS)),
            dma((3 + CROSSED, CHUNKS)),
            dma((8,)),
            dma((8,)),
            dma((CHUNKS,)),
            dma((CHUNKS,)),
            dma((2, CHUNKS, 8)),
            dma((2, CHUNKS, 8)),
            dma((CHUNKS,)),
            dma((CHUNKS,)),
            dma((CHUNKS, 4)),
            dma((CHUNKS, 4)),
            dma((2,)),
            dma((2,)),
            dma((5,)),
        ],
        compiler_params=pltpu.CompilerParams(
            collective_id=0, has_side_effects=True, vmem_limit_bytes=63 * 2**20
        ),
        cost_estimate=pl.CostEstimate(
            flops=12 * slots * width * hidden,
            bytes_accessed=2 * (6 * width * hidden + 2 * slots * hidden + 4 * count * width),
            transcendentals=slots * hidden,
        ),
    )(
        routing.reshape(1, count),
        tokens,
        out_grad,
        router_weight.T,
        gate_weight[0],
        up_weight[0],
        down_weight[0],
        saved_gate[0],
        saved_up[0],
    )
    grad_tokens, early, late_in, late_grad, grad_down, grad_router = outs
    grad_gate, grad_up, grad_tokens, grad_down, grad_router = pl.pallas_call(
        finish,
        out_shape=(
            jax.ShapeDtypeStruct((width, hidden), BF16),
            jax.ShapeDtypeStruct((width, hidden), BF16),
            jax.ShapeDtypeStruct((count, width), BF16),
            jax.ShapeDtypeStruct((hidden, width), BF16),
            jax.ShapeDtypeStruct((experts, width), F32),
        ),
        in_specs=[anywhere] * 6,
        out_specs=(anywhere,) * 5,
        scratch_shapes=[
            pltpu.VMEM((width, 2 * hidden), BF16),
            pltpu.VMEM((per, width), BF16),
            pltpu.VMEM((per, 2 * hidden), BF16),
            pltpu.VMEM((count, width), BF16),
            pltpu.VMEM((hidden, width), BF16),
            pltpu.VMEM((experts, width), F32),
            pltpu.VMEM((width, hidden), BF16),
            pltpu.VMEM((width, hidden), BF16),
            dma((10,)),
            dma((13,)),
        ],
        compiler_params=pltpu.CompilerParams(vmem_limit_bytes=62 * 2**20),
    )(early, late_in.reshape(per, width), late_grad, grad_tokens, grad_down, grad_router)
    return grad_tokens, grad_gate[None], grad_up[None], grad_down[None], grad_router.T


def solution(mesh):
    placed = (
        P(("dp", "tensor"), None),
        P(("dp", "tensor"), None),
        P(("dp", "tensor"), None),
        P(),
        P("dp", None, "tensor"),
        P("dp", None, "tensor"),
        P("dp", "tensor", None),
        P("dp", None, "tensor"),
        P("dp", None, "tensor"),
    )
    return jax.shard_map(
        local,
        mesh=mesh,
        in_specs=placed,
        out_specs=(
            P(("dp", "tensor"), None),
            P("dp", None, "tensor"),
            P("dp", None, "tensor"),
            P("dp", "tensor", None),
            P(),
        ),
        check_vma=False,
    )
```
